256 devices in a mesh: context: 32 (over x, z), tensor: 8 (over y, core).
Axes of the slice: x: 4, y: 4, z: 8, core: 2. Of those that a mesh axis runs over, the one named last changes fastest.
Arguments:
- first_input: bfloat16 [16, 5376], P(None, 'context'), may hold values from -13 to 13
- second_input: bfloat16 [16, 5376], P(None, 'context'), may hold values from -13 to 13
- attn_gain: bfloat16 [5376], P('context'), may hold values from 0.099609375 to 1.8984375
- query_weight: bfloat16 [5376, 4096], P('context', 'tensor'), may hold values from -0.078125 to 0.078125
- key_weight: bfloat16 [5376, 2048], P('context', 'tensor'), may hold values from -0.25 to 0.25
- value_weight: bfloat16 [5376, 2048], P('context', 'tensor'), may hold values from -0.078125 to 0.078125
- out_weight: bfloat16 [4096, 5376], P('tensor', 'context'), may hold values from -0.09375 to 0.09375
- ffn_gain: bfloat16 [5376], P('context'), may hold values from 0.099609375 to 1.8984375
- gate_weight: bfloat16 [5376, 21504], P('context', 'tensor'), may hold values from -0.078125 to 0.078125
- up_weight: bfloat16 [5376, 21504], P('context', 'tensor'), may hold values from -0.078125 to 0.078125
- down_weight: bfloat16 [21504, 5376], P('tensor', 'context'), may hold values from -0.0625 to 0.0625
- key_cache: bfloat16 [16, 16384, 16, 128], P(None, 'context', 'tensor'), may hold values from -320 to 320
- value_cache: bfloat16 [16, 16384, 16, 128], P(None, 'context', 'tensor'), may hold values from -6 to 6
- lengths: int32 [16], replicated, may hold values from 1 to 16384, as said below
- granularity: int32 [16], replicated, may hold values from 1 to 8, as said below
Outputs:
- first_output: bfloat16 [16, 5376], P(None, 'context')
- second_output: bfloat16 [16, 5376], P(None, 'context')
The draws below stay inside these ranges and needn't reach their ends.
Inputs may be any that keep to these rules, and one draw needn't show every extreme that they name: `lengths`: some request has all 16384 positions live. `granularity`: some request uses all 8 granularities.
All inputs are finite; a program needn't handle non-finite values.
Results may differ from the reference program's by a relative error of at most 0.0118.
Values may be sent and summed in bfloat16 or wider, within the bound.
A program may use at most 64 MiB of HBM per device.

```python
import math
import jax
import jax.numpy as jnp
from jax import lax

D = 5376
HEADS = 32
KV_HEADS = 16
HEAD = 128
FF = 21504
LEVELS = 8
REQS = 16
CTX_DEV = 512
LEN = 16384
N_CONTEXT = 32


def shaped_rows(base_draw, row_key, column_spread, row_low, row_high):
    column_ramp = jnp.exp(math.log(column_spread) * jnp.arange(D, dtype=jnp.float32) / D)
    norm_const = math.sqrt((column_spread * column_spread - 1.0) / (2.0 * math.log(column_spread)))
    row_scale = row_low * jnp.exp(math.log(row_high / row_low) * jax.random.uniform(row_key, (REQS, 1), jnp.float32))
    return base_draw * (column_ramp / norm_const)[None, :] * row_scale


def draw_first_input(key, part):
    key = jax.random.fold_in(key, 3)
    base_key, row_key = jax.random.split(key)
    base_draw = jnp.clip(jax.random.normal(base_key, (REQS, D), jnp.float32), -5.0, 5.0)
    return shaped_rows(base_draw, row_key, 3.0, 0.6, 1.6).astype(jnp.bfloat16)


def draw_second_input(key, part):
    key = jax.random.fold_in(key, 4)
    base_key, row_key = jax.random.split(key)
    base_draw = jnp.clip(jax.random.normal(base_key, (REQS, D), jnp.float32), -5.0, 5.0)
    return shaped_rows(base_draw, row_key, 3.0, 0.6, 1.6).astype(jnp.bfloat16)


def draw_key_cache(key, part):
    key = jax.random.fold_in(key, 11)
    shape_all = (REQS, LEN, KV_HEADS, HEAD)
    base_key = jax.random.fold_in(key, 0)
    return jnp.clip(jax.random.normal(base_key, shape_all, jnp.float32) * 3.0, -24.0, 24.0).astype(jnp.bfloat16)


def draw_lengths(key, part):
    key = jax.random.fold_in(key, 5)
    power_key, length_key, full_key = jax.random.split(key, 3)
    top_power = int(math.ceil(math.log2(LEN))) + 1
    exponent = jax.random.randint(power_key, (REQS,), 0, top_power)
    span_max = jnp.minimum(LEN, jnp.left_shift(jnp.ones_like(exponent), exponent))
    drawn = 1 + jax.random.randint(length_key, (REQS,), 0, span_max)
    full_index = jax.random.randint(full_key, (), 0, REQS)
    return jnp.where(jnp.arange(REQS, dtype=jnp.int32) == full_index, LEN, drawn).astype(jnp.int32)


def draw_granularity(key, part):
    key = jax.random.fold_in(key, 7)
    level_key, full_key = jax.random.split(key)
    drawn = jax.random.randint(level_key, (REQS,), 1, LEVELS + 1)
    full_index = jax.random.randint(full_key, (), 0, REQS)
    return jnp.where(jnp.arange(REQS, dtype=jnp.int32) == full_index, LEVELS, drawn).astype(jnp.int32)


def steps_of(key, dims, pieces, low, largest):
    def one(dim, parts):
        steps = jax.random.uniform(jax.random.fold_in(jax.random.fold_in(key, 6), dim), (parts,), jnp.float32, low / len(pieces), largest / len(pieces))
        return jnp.repeat(jnp.exp(steps), dims[dim] // parts).reshape((-1,) + (1,) * (len(dims) - dim - 1))

    factor_of = one(*pieces[0])
    for cut in pieces[1:]:
        factor_of = factor_of * one(*cut)
    return factor_of


def centred(key, dims, spread, reach, shards=(), kind=jnp.bfloat16):
    values = jax.random.normal(key, dims, jnp.float32) * spread
    if len(shards) > 0:
        values = steps_of(key, dims, shards, -0.22, 0.18) * values
    return jnp.clip(values, min=-reach, max=reach).astype(kind)


def setup_inputs(seed: int = 0) -> dict:
    seeds = jax.random.split(jax.random.key(seed), 16)
    return {
        "first_input": draw_first_input(jax.random.fold_in(seeds[15], 71), 0),
        "second_input": draw_second_input(jax.random.fold_in(seeds[15], 71), 0),
        "attn_gain": jnp.clip(1.0 + 0.18 * jax.random.normal(seeds[2], (D,), jnp.float32), 0.099609375, 1.8984375).astype(jnp.bfloat16),
        "query_weight": centred(seeds[3], (D, HEADS * HEAD), D ** -0.5, 0.078125, ((0, 32), (1, 8))),
        "key_weight": centred(seeds[4], (D, KV_HEADS * HEAD), (D // 9) ** -0.5, 0.25, ((0, 32), (1, 8))),
        "value_weight": centred(seeds[5], (D, KV_HEADS * HEAD), D ** -0.5, 0.078125, ((0, 32), (1, 8))),
        "out_weight": centred(seeds[6], (HEADS * HEAD, D), (HEADS * HEAD) ** -0.5, 0.09375, ((0, 8), (1, 32))),
        "ffn_gain": jnp.clip(1.0 + 0.18 * jax.random.normal(seeds[7], (D,), jnp.float32), 0.099609375, 1.8984375).astype(jnp.bfloat16),
        "gate_weight": centred(seeds[8], (D, FF), D ** -0.5, 0.078125, ((0, 32), (1, 8))),
        "up_weight": centred(seeds[9], (D, FF), D ** -0.5, 0.078125, ((0, 32), (1, 8))),
        "down_weight": centred(seeds[10], (FF, D), (FF // 2) ** -0.5, 0.0625, ((0, 8), (1, 32))),
        "key_cache": draw_key_cache(jax.random.fold_in(seeds[15], 71), 0),
        "value_cache": centred(seeds[12], (REQS, LEN, KV_HEADS, HEAD), 1.0, 6.0, ((1, 32), (2, 8))),
        "lengths": draw_lengths(jax.random.fold_in(seeds[15], 71), 0),
        "granularity": draw_granularity(jax.random.fold_in(seeds[15], 71), 0),
    }


EPS = 1e-06
MASKED = -1e+30

def inverse_rms(values):
    mean_square = lax.optimization_barrier(jnp.mean(values * values, axis=1, keepdims=True))
    return lax.rsqrt(mean_square + EPS)

def cache_partials(queries, key_cache, value_cache, lengths):
    score_scale = HEAD ** (-0.5)
    query_f32 = queries.astype(jnp.float32)

    def one_block(block_index):
        first_pos = block_index * CTX_DEV
        keys_block = lax.dynamic_slice_in_dim(key_cache, first_pos, CTX_DEV, 1).astype(jnp.float32)
        values_block = lax.dynamic_slice_in_dim(value_cache, first_pos, CTX_DEV, 1).astype(jnp.float32)
        positions = first_pos + jnp.arange(CTX_DEV, dtype=jnp.int32)
        live_keys = (positions[None, :] < lengths[:, None])[:, None, None, :]
        scores = jnp.einsum('rkge,rpke->rkgp', query_f32, keys_block) * score_scale
        local_peak = lax.optimization_barrier(jnp.max(jnp.where(live_keys, scores, MASKED), axis=3))
        weights = jnp.where(live_keys, jnp.exp(scores - local_peak[..., None]), 0.0)
        totals = lax.optimization_barrier(jnp.sum(weights, axis=3))
        rounded = lax.optimization_barrier(weights.astype(jnp.bfloat16))
        mixture = jnp.einsum('rkgp,rpke->rkge', rounded.astype(jnp.float32), values_block)
        return (local_peak, totals, mixture)
    return lax.map(one_block, jnp.arange(N_CONTEXT, dtype=jnp.int32))

def decode_step(inputs, earlier, params):
    attn_gain, query_weight, key_weight, value_weight, out_weight, ffn_gain, gate_weight, up_weight, down_weight, key_cache, value_cache, lengths, granularity = params
    group_size = HEADS // KV_HEADS
    rows_f32 = inputs.astype(jnp.float32)
    gated = (rows_f32 * attn_gain.astype(jnp.float32)).astype(jnp.bfloat16)
    row_inv = inverse_rms(rows_f32)
    queries = (jnp.dot(gated, query_weight, preferred_element_type=jnp.float32) * row_inv).astype(jnp.bfloat16)
    queries = queries.reshape(REQS, KV_HEADS, group_size, HEAD)
    new_key = (jnp.dot(gated, key_weight, preferred_element_type=jnp.float32) * row_inv).astype(jnp.bfloat16)
    new_value = (jnp.dot(gated, value_weight, preferred_element_type=jnp.float32) * row_inv).astype(jnp.bfloat16)
    extras = earlier + [(new_key.reshape(REQS, KV_HEADS, HEAD), new_value.reshape(REQS, KV_HEADS, HEAD))]
    block_peaks, totals, mixture = cache_partials(queries, key_cache, value_cache, lengths)
    query_f32 = queries.astype(jnp.float32)
    own_list = [jnp.einsum('rkge,rke->rkg', query_f32, key_item.astype(jnp.float32)) * HEAD ** (-0.5) for key_item, value_item in extras]
    highest = lax.optimization_barrier(jnp.max(block_peaks, axis=0))
    for own_score in own_list:
        highest = jnp.maximum(highest, own_score)
    rescale = jnp.exp(block_peaks - highest[None])
    denominator = lax.optimization_barrier(jnp.sum(rescale * totals, axis=0))
    numerator = lax.optimization_barrier(jnp.sum(rescale[..., None] * mixture, axis=0))
    for own_score, pair_item in zip(own_list, extras):
        own_weight = jnp.exp(own_score - highest)
        denominator = denominator + own_weight
        numerator = numerator + own_weight[..., None] * pair_item[1].astype(jnp.float32)[:, :, None, :]
    attended = (numerator / denominator[..., None]).astype(jnp.bfloat16).reshape(REQS, HEADS * HEAD)
    residual = rows_f32 + jnp.dot(attended, out_weight, preferred_element_type=jnp.float32)
    ffn_gated = (residual * ffn_gain.astype(jnp.float32)).astype(jnp.bfloat16)
    ffn_inv = inverse_rms(residual)
    gate_sum = jnp.dot(ffn_gated, gate_weight, preferred_element_type=jnp.float32) * ffn_inv
    up_sum = jnp.dot(ffn_gated, up_weight, preferred_element_type=jnp.float32) * ffn_inv
    columns = jnp.arange(FF, dtype=jnp.int32)
    active = columns[None, :] < granularity[:, None] * (FF // LEVELS)
    hidden = jnp.where(active, jax.nn.gelu(gate_sum, approximate=True) * up_sum, 0.0).astype(jnp.bfloat16)
    output = (residual + jnp.dot(hidden, down_weight, preferred_element_type=jnp.float32)).astype(jnp.bfloat16)
    return (output, extras)

def reference(first_input, second_input, attn_gain, query_weight, key_weight, value_weight, out_weight, ffn_gain, gate_weight, up_weight, down_weight, key_cache, value_cache, lengths, granularity):
    params = (attn_gain, query_weight, key_weight, value_weight, out_weight, ffn_gain, gate_weight, up_weight, down_weight, key_cache, value_cache, lengths, granularity)
    first_output, extras = decode_step(first_input, [], params)
    second_output, unused_extras = decode_step(second_input, extras, params)
    return (first_output, second_output)
```

```python
import math

import jax
import jax.numpy as jnp
from jax import lax
from jax.experimental import pallas as pl
from jax.experimental.pallas import tpu as pltpu
from jax.sharding import PartitionSpec as P

EPS = 1e-06
MASKED = -1e30
WIDTH = 5376
COLS = 168
HEAD = 128
CTX = 32
TEN = 8
REQS = 16
ROWS = 32
POS = 512
TILES = 21
EXTRA = 10
SCALE = HEAD**-0.5
GELU = math.sqrt(2.0 / math.pi)
MESH = pl.DeviceIdType.MESH
F32 = jnp.float32
BF16 = jnp.bfloat16

N_LOCAL = 15


def iota(shape, dim):
    return lax.broadcasted_iota(jnp.int32, shape, dim)


def peer_of(x, z, i):
    zi, xi = i // 4, i % 4
    zo = 4 + ((zi + 1) // 2) * (1 - 2 * (zi % 2))
    xo = 2 + ((xi + 1) // 2) * (1 - 2 * (xi % 2))
    return lax.rem(x + xo, 4) * 8 + lax.rem(z + zo, 8)


def nt_dot(a, b):
    return lax.dot_general(a, b, (((1,), (1,)), ((), ())), preferred_element_type=F32)


def kernel(
    lengths,
    granularity,
    x1_hbm,
    x2_hbm,
    gains_hbm,
    wq_hbm,
    wk_hbm,
    wv_hbm,
    wo_hbm,
    wg_hbm,
    wu_hbm,
    wd_hbm,
    kc_hbm,
    vc_hbm,
    o1_ref,
    o2_ref,
    x1,
    x2,
    gains,
    wq,
    wk,
    wv,
    wo,
    wg,
    wu,
    wd,
    kc,
    vc,
    qkv_out,
    qkv_in,
    qkv_all,
    mix_out,
    mix_in,
    att_all,
    proj_out,
    proj_in,
    sq_out,
    sq_in,
    gu_out,
    gu_in,
    gu_in2,
    hid_all,
    down_in,
    local_sem,
    send_sem,
    recv_sem,
):
    c = lax.axis_index("context")
    t = lax.axis_index("tensor")
    x, z = c // 8, c % 8

    def local(i, src, dst):
        return pltpu.make_async_copy(src, dst, local_sem.at[i])

    loads = [
        local(0, x1_hbm, x1),
        local(1, x2_hbm, x2),
        local(2, gains_hbm, gains),
        local(3, wq_hbm, wq),
        local(4, wk_hbm, wk),
        local(5, wv_hbm, wv),
        local(6, kc_hbm, kc),
        local(7, vc_hbm, vc),
        local(8, wo_hbm, wo),
        local(9, wg_hbm, wg),
        local(10, wu_hbm, wu),
        local(11, wd_hbm, wd),
    ]
    for load in loads:
        load.start()

    barrier = pltpu.get_barrier_semaphore()

    @pl.loop(0, CTX - 1)
    def _(i):
        pl.semaphore_signal(
            barrier, inc=1, device_id=(peer_of(x, z, i), t), device_id_type=MESH
        )

    @pl.loop(1, TEN)
    def _(d):
        pl.semaphore_signal(
            barrier, inc=1, device_id=(c, lax.rem(t + d, TEN)), device_id_type=MESH
        )

    def send(phase, src, dst, peer):
        pltpu.make_async_remote_copy(
            src_ref=src,
            dst_ref=dst,
            send_sem=send_sem.at[phase],
            recv_sem=recv_sem.at[phase],
            device_id=peer,
            device_id_type=MESH,
        ).start()

    def wait(sem, ref):
        pltpu.make_async_copy(ref, ref, sem).wait()

    for i in range(6):
        loads[i].wait()
    rows = jnp.concatenate([x1[...], x2[...]], axis=0).astype(F32)
    gated = (rows * gains[0:1, :]).astype(BF16)
    q_part = jnp.dot(gated, wq[...], preferred_element_type=F32)
    k_part = jnp.dot(gated, wk[...], preferred_element_type=F32)
    v_part = jnp.dot(gated, wv[...], preferred_element_type=F32)
    part = jnp.concatenate([q_part, k_part, v_part], axis=1)
    square = jnp.sum(rows * rows, axis=1, keepdims=True)
    square_hi = square.astype(BF16).astype(F32)
    square_tile = jnp.where(iota((ROWS, HEAD), 1) == 0, square_hi, square - square_hi)
    for j in range(8):
        for g in range(4):
            tile = jnp.concatenate(
                [
                    part[g * 8 : g * 8 + 8, j * HEAD : (j + 1) * HEAD],
                    square_tile[g * 8 : g * 8 + 8, :],
                ],
                axis=0,
            )
            qkv_out[j * 4 + g] = tile.astype(BF16)

    pl.semaphore_wait(barrier, CTX - 1 + TEN - 1)

    @pl.loop(0, CTX - 1)
    def _(i):
        p = peer_of(x, z, i)
        send(0, qkv_out.at[p], qkv_in.at[i], (p, t))

    qkv_in[CTX - 1] = qkv_out[c]
    wait(recv_sem.at[0], qkv_in.at[pl.ds(0, CTX - 1)])
    total = jnp.sum(qkv_in[...].astype(F32), axis=0)
    squares = total[8:16, 0:1] + total[8:16, 1:2]
    inv = lax.rsqrt(squares / WIDTH + EPS)
    mine = pl.multiple_of(c * 8, 8)
    qkv_all[pl.ds(mine, 8), :] = (total[0:8, :] * inv).astype(BF16).astype(F32)

    @pl.loop(0, CTX - 1)
    def _(i):
        tile = qkv_all.at[pl.ds(mine, 8)]
        send(1, tile, tile, (peer_of(x, z, i), t))

    wait(recv_sem.at[1], qkv_all.at[pl.ds(0, 8 * (CTX - 1))])

    loads[6].wait()
    loads[7].wait()
    lane = iota((8, 2 * POS), 1)
    own_head = (lane % 2) == (iota((8, 2 * POS), 0) // 4)
    position = c * POS + lane // 2

    @pl.loop(0, REQS)
    def _(r):
        queries = qkv_all[pl.ds(r, 8, stride=16), :].astype(BF16)
        scores = nt_dot(queries, kc[r]) * SCALE
        live = own_head & (position < lengths[r])
        peak = jnp.max(jnp.where(live, scores, MASKED), axis=1, keepdims=True)
        weights = jnp.where(live, jnp.exp(scores - peak), 0.0)
        sums = jnp.sum(weights, axis=1, keepdims=True)
        mixture = jnp.dot(weights.astype(BF16), vc[r], preferred_element_type=F32)
        stats = jnp.where(iota((8, HEAD), 1) < 64, peak, sums)
        mix_out[2 * r] = jnp.concatenate([mixture[0:4], stats[0:4]], axis=0)
        mix_out[2 * r + 1] = jnp.concatenate([mixture[4:8], stats[4:8]], axis=0)

    @pl.loop(0, CTX - 1)
    def _(i):
        p = peer_of(x, z, i)
        send(2, mix_out.at[p], mix_in.at[i], (p, t))

    mix_in[CTX - 1] = mix_out[c]
    request, kv = c // 2, c % 2

    def new_row(j, s):
        return qkv_all[pl.ds(j * 32 + s * 16 + request, 1), :]

    query = jnp.concatenate([new_row(2 * kv + m // 2, m % 2) for m in range(4)], axis=0)
    own = [
        jnp.sum(query * new_row(4 + kv, s), axis=1, keepdims=True) * SCALE for s in range(2)
    ]
    second = (iota((4, 1), 0) % 2) == 1
    own[1] = jnp.where(second, own[1], MASKED)
    wait(recv_sem.at[2], mix_in.at[pl.ds(0, CTX - 1)])
    mixed = mix_in[:, 0:4, :]
    peaks = mix_in[:, 4:8, 0:1]
    sums = mix_in[:, 4:8, 64:65]
    highest = jnp.maximum(jnp.max(peaks, axis=0), jnp.maximum(own[0], own[1]))
    rescale = jnp.exp(peaks - highest[None])
    denominator = jnp.sum(rescale * sums, axis=0)
    numerator = jnp.sum(rescale * mixed, axis=0)
    own_weight = [jnp.exp(own[0] - highest), jnp.where(second, jnp.exp(own[1] - highest), 0.0)]
    for s in range(2):
        denominator = denominator + own_weight[s]
        numerator = numerator + own_weight[s] * new_row(6 + kv, s)
    attended = (numerator / denominator).astype(BF16).astype(F32)
    att_all[pl.ds(mine, 8), :] = jnp.concatenate([attended, attended], axis=0)

    @pl.loop(0, CTX - 1)
    def _(i):
        tile = att_all.at[pl.ds(mine, 8)]
        send(3, tile, tile, (peer_of(x, z, i), t))

    loads[8].wait()
    wait(recv_sem.at[3], att_all.at[pl.ds(0, 8 * (CTX - 1))])

    att = jnp.concatenate(
        [
            jnp.concatenate(
                [
                    att_all[pl.ds((j // 2) * 8 + (j % 2) * 2 + s, REQS, stride=16), :]
                    for s in range(2)
                ],
                axis=0,
            )
            for j in range(4)
        ],
        axis=1,
    ).astype(BF16)
    pad = jnp.zeros((ROWS, 2 * HEAD - COLS), F32)

    def over_tensor(phase, value, slots):
        proj_out[phase - 4] = jnp.concatenate([value, pad], axis=1).astype(BF16)

        @pl.loop(1, TEN)
        def _(d):
            send(phase, proj_out.at[phase - 4], slots.at[t], (c, lax.rem(t + d, TEN)))

        slots[t] = proj_out[phase - 4]
        wait(recv_sem.at[phase], slots.at[pl.ds(0, TEN - 1)])
        return jnp.sum(slots[...].astype(F32), axis=0)[:, 0:COLS]

    residual = rows + over_tensor(4, nt_dot(att, wo[...]), proj_in)

    square = jnp.sum(residual * residual, axis=1, keepdims=True)
    diagonal = iota((ROWS, HEAD), 0) == iota((ROWS, HEAD), 1)
    sq_out[...] = jnp.sum(jnp.where(diagonal, square, 0.0), axis=0, keepdims=True)

    @pl.loop(0, CTX - 1)
    def _(i):
        send(6, sq_out, sq_in.at[i], (peer_of(x, z, i), t))

    sq_in[CTX - 1] = sq_out[...]
    ffn_gated = (residual * gains[1:2, :]).astype(BF16)
    loads[9].wait()
    loads[10].wait()

    @pl.loop(0, 7)
    def _(n):
        columns = pl.ds(pl.multiple_of(n * 384, 384), 384)
        gate = jnp.dot(ffn_gated, wg[:, columns], preferred_element_type=F32).astype(BF16)
        up = jnp.dot(ffn_gated, wu[:, columns], preferred_element_type=F32).astype(BF16)
        for k in range(3):
            for s in range(2):
                unit = 6 * n + 2 * k + s
                gu_out[unit, 0:16, :] = gate[s * 16 : s * 16 + 16, k * HEAD : (k + 1) * HEAD]
                gu_out[unit, 16:32, :] = up[s * 16 : s * 16 + 16, k * HEAD : (k + 1) * HEAD]

    @pl.loop(0, CTX - 1)
    def _(i):
        p = peer_of(x, z, i)
        send(7, gu_out.at[p], gu_in.at[i], (p, t))

    @pl.loop(0, EXTRA)
    def _(p):
        @pl.when(p != c)
        def _():
            send(8, gu_out.at[CTX + p], gu_in2.at[c], (p, t))

    gu_in[CTX - 1] = gu_out[c]

    wait(recv_sem.at[6], sq_in.at[pl.ds(0, CTX - 1)])
    squares = jnp.sum(sq_in[...], axis=0)
    step_rows = iota((REQS, HEAD), 1) == iota((REQS, HEAD), 0) + REQS * (c % 2)
    squares = jnp.sum(jnp.where(step_rows, squares, 0.0), axis=1, keepdims=True)
    ffn_inv = lax.rsqrt(squares / WIDTH + EPS)
    levels = jnp.zeros((REQS, 1), jnp.int32)
    for r in range(REQS):
        levels = jnp.where(iota((REQS, 1), 0) == r, granularity[r], levels)
    active = levels > t

    def hidden_of(slots):
        both = jnp.sum(slots[...].astype(F32), axis=0)
        gate = both[0:16] * ffn_inv
        up = both[16:32] * ffn_inv
        act = 0.5 * gate * (1.0 + jnp.tanh(GELU * (gate + 0.044715 * (gate * gate * gate))))
        return jnp.where(active, act * up, 0.0).astype(BF16)

    def share(phase, unit):
        part_of = hid_all.at[pl.ds(pl.multiple_of(unit * 16, 16), 16)]

        @pl.loop(0, CTX - 1)
        def _(i):
            send(phase, part_of, part_of, (peer_of(x, z, i), t))

    wait(recv_sem.at[7], gu_in.at[pl.ds(0, CTX - 1)])
    hid_all[pl.ds(pl.multiple_of(c * 16, 16), 16), :] = hidden_of(gu_in)
    share(9, c)

    @pl.when(c < EXTRA)
    def _():
        gu_in2[c] = gu_out[CTX + c]
        wait(recv_sem.at[8], gu_in2.at[pl.ds(0, CTX - 1)])
        hid_all[pl.ds(pl.multiple_of((CTX + c) * 16, 16), 16), :] = hidden_of(gu_in2)
        share(10, CTX + c)

    loads[11].wait()
    wait(recv_sem.at[9], hid_all.at[pl.ds(0, 16 * (CTX - 1))])

    @pl.when(c < EXTRA)
    def _():
        wait(recv_sem.at[10], hid_all.at[pl.ds(0, 16 * (EXTRA - 1))])

    @pl.when(c >= EXTRA)
    def _():
        wait(recv_sem.at[10], hid_all.at[pl.ds(0, 16 * EXTRA)])

    hidden = jnp.concatenate(
        [hid_all[i * ROWS : (i + 1) * ROWS, :] for i in range(TILES)], axis=1
    )
    output = residual + over_tensor(5, nt_dot(hidden, wd[...]), down_in)
    output = output.astype(BF16)
    o1_ref[...] = output[0:REQS]
    o2_ref[...] = output[REQS:ROWS]

    wait(send_sem.at[0], qkv_in.at[pl.ds(0, CTX - 1)])
    wait(send_sem.at[1], qkv_all.at[pl.ds(0, 8 * (CTX - 1))])
    wait(send_sem.at[2], mix_in.at[pl.ds(0, CTX - 1)])
    wait(send_sem.at[3], att_all.at[pl.ds(0, 8 * (CTX - 1))])
    wait(send_sem.at[4], proj_in.at[pl.ds(0, TEN - 1)])
    wait(send_sem.at[5], down_in.at[pl.ds(0, TEN - 1)])
    wait(send_sem.at[6], sq_in.at[pl.ds(0, CTX - 1)])
    wait(send_sem.at[7], gu_in.at[pl.ds(0, CTX - 1)])

    wait(send_sem.at[9], hid_all.at[pl.ds(0, 16 * (CTX - 1))])

    @pl.when(c < EXTRA)
    def _():
        wait(send_sem.at[8], gu_in.at[pl.ds(0, EXTRA - 1)])
        wait(send_sem.at[10], hid_all.at[pl.ds(0, 16 * (CTX - 1))])

    @pl.when(c >= EXTRA)
    def _():
        wait(send_sem.at[8], gu_in.at[pl.ds(0, EXTRA)])


def per_device(
    first_input,
    second_input,
    attn_gain,
    query_weight,
    key_weight,
    value_weight,
    out_weight,
    ffn_gain,
    gate_weight,
    up_weight,
    down_weight,
    key_cache,
    value_cache,
    lengths,
    granularity,
):
    gains = jnp.stack([attn_gain, ffn_gain]).astype(F32)
    any_space = pl.BlockSpec(memory_space=pl.ANY)
    smem = pl.BlockSpec(memory_space=pltpu.SMEM)
    vmem = pl.BlockSpec(memory_space=pltpu.VMEM)
    V = pltpu.VMEM
    return pl.pallas_call(
        kernel,
        out_shape=(
            jax.ShapeDtypeStruct((REQS, COLS), BF16),
            jax.ShapeDtypeStruct((REQS, COLS), BF16),
        ),
        in_specs=[smem, smem] + [any_space] * 12,
        out_specs=(vmem, vmem),
        scratch_shapes=[
            V((REQS, COLS), BF16),
            V((REQS, COLS), BF16),
            V((2, COLS), F32),
            V((COLS, 512), BF16),
            V((COLS, 256), BF16),
            V((COLS, 256), BF16),
            V((COLS, 512), BF16),
            V((COLS, 2688), BF16),
            V((COLS, 2688), BF16),
            V((COLS, 2688), BF16),
            V((REQS, 2 * POS, HEAD), BF16),
            V((REQS, 2 * POS, HEAD), BF16),
            V((CTX, 16, HEAD), BF16),
            V((CTX, 16, HEAD), BF16),
            V((CTX * 8, HEAD), F32),
            V((CTX, 8, HEAD), F32),
            V((CTX, 8, HEAD), F32),
            V((CTX * 8, HEAD), F32),
            V((2, ROWS, 2 * HEAD), BF16),
            V((TEN, ROWS, 2 * HEAD), BF16),
            V((1, HEAD), F32),
            V((CTX, 1, HEAD), F32),
            V((2 * TILES, 32, HEAD), BF16),
            V((CTX, 32, HEAD), BF16),
            V((CTX, 32, HEAD), BF16),
            V((TILES * ROWS, HEAD), BF16),
            V((TEN, ROWS, 2 * HEAD), BF16),
            pltpu.SemaphoreType.DMA((12,)),
            pltpu.SemaphoreType.DMA((11,)),
            pltpu.SemaphoreType.DMA((11,)),
        ],
        compiler_params=pltpu.CompilerParams(
            collective_id=0, has_side_effects=True, vmem_limit_bytes=40 * 2**20
        ),
    )(
        lengths,
        granularity,
        first_input,
        second_input,
        gains,
        query_weight,
        key_weight,
        value_weight,
        out_weight.T,
        gate_weight,
        up_weight,
        down_weight.T,
        key_cache.reshape(REQS, 2 * POS, HEAD),
        value_cache.reshape(REQS, 2 * POS, HEAD),
    )


def solution(mesh):
    return jax.shard_map(
        per_device,
        mesh=mesh,
        in_specs=(
            P(None, "context"),
            P(None, "context"),
            P("context"),
            P("context", "tensor"),
            P("context", "tensor"),
            P("context", "tensor"),
            P("tensor", "context"),
            P("context"),
            P("context", "tensor"),
            P("context", "tensor"),
            P("tensor", "context"),
            P(None, "context", "tensor", None),
            P(None, "context", "tensor", None),
            P(),
            P(),
        ),
        out_specs=(P(None, "context"), P(None, "context")),
        check_vma=False,
    )
```

```python
import math

import jax
import jax.numpy as jnp
from jax import lax
from jax.experimental import pallas as pl
from jax.experimental.pallas import tpu as pltpu
from jax.sharding import PartitionSpec as P

EPS = 1e-06
MASKED = -1e30
WIDTH = 5376
COLS = 168
HEAD = 128
CTX = 32
TEN = 8
REQS = 16
ROWS = 32
POS = 512
TILES = 21
EXTRA = 10
SCALE = HEAD**-0.5
GELU = math.sqrt(2.0 / math.pi)
MESH = pl.DeviceIdType.MESH
F32 = jnp.float32
BF16 = jnp.bfloat16


def iota(shape, dim):
    return lax.broadcasted_iota(jnp.int32, shape, dim)


def ring_peer(me, i, size=8):
    return lax.rem(me + size // 2 + ((i + 1) // 2) * (1 - 2 * (i % 2)), size)


def peer_of(x, z, i):
    return ring_peer(x, i % 4, 4) * 8 + ring_peer(z, i // 4)


def nt_dot(a, b):
    return lax.dot_general(a, b, (((1,), (1,)), ((), ())), preferred_element_type=F32)


def kernel(
    lengths_hbm,
    granularity_hbm,
    x1_hbm,
    x2_hbm,
    gain1_hbm,
    gain2_hbm,
    wq_hbm,
    wk_hbm,
    wv_hbm,
    wo_hbm,
    wg_hbm,
    wu_hbm,
    wd_hbm,
    kc_hbm,
    vc_hbm,
    o1_ref,
    o2_ref,
    lengths,
    granularity,
    x1,
    x2,
    gain1,
    gain2,
    wq,
    wk,
    wv,
    wo,
    wg,
    wu,
    wd,
    kc,
    vc,
    qkv_out,
    qkv_in,
    qkv_all,
    mix_out,
    mix_in,
    att_all,
    proj_out,
    proj_in,
    sq_out,
    sq_in,
    gu_out,
    gx_in,
    gz_out,
    gz_in,
    gz_in2,
    hid_all,
    down_in,
    local_sem,
    send_sem,
    recv_sem,
    gx_send,
    gx_recv,
    gz_send,
):
    c = lax.axis_index("context")
    t = lax.axis_index("tensor")
    x, z = c // 8, c % 8

    def local(i, src, dst):
        return pltpu.make_async_copy(src, dst, local_sem.at[i])

    loads = [
        local(0, x1_hbm, x1),
        local(1, x2_hbm, x2),
        local(2, gain1_hbm, gain1),
        local(3, wq_hbm, wq),
        local(4, wk_hbm, wk),
        local(5, wv_hbm, wv),
        local(6, kc_hbm, kc),
        local(7, vc_hbm, vc),
        local(8, wo_hbm, wo),
        local(9, wg_hbm, wg),
        local(10, wu_hbm, wu),
        local(11, wd_hbm, wd),
        local(12, gain2_hbm, gain2),
        local(13, lengths_hbm, lengths),
        local(14, granularity_hbm, granularity),
    ]
    barrier = pltpu.get_barrier_semaphore()

    @pl.loop(0, CTX - 1)
    def _(i):
        pl.semaphore_signal(
            barrier, inc=1, device_id=(peer_of(x, z, i), t), device_id_type=MESH
        )

    @pl.loop(0, TEN - 1)
    def _(i):
        pl.semaphore_signal(
            barrier, inc=1, device_id=(c, ring_peer(t, i)), device_id_type=MESH
        )

    for load in loads:
        load.start()

    def send(phase, src, dst, peer):
        pltpu.make_async_remote_copy(
            src_ref=src,
            dst_ref=dst,
            send_sem=send_sem.at[phase],
            recv_sem=recv_sem.at[phase],
            device_id=peer,
            device_id_type=MESH,
        ).start()

    def wait(sem, ref):
        pltpu.make_async_copy(ref, ref, sem).wait()

    left = []

    def leaves(phase, ref):
        left.append(lambda: wait(send_sem.at[phase], ref))

    for i in range(6):
        loads[i].wait()
    rows = jnp.concatenate([x1[...], x2[...]], axis=0).astype(F32)
    gated = (rows * gain1[...].astype(F32)[None, :]).astype(BF16)
    q_part = jnp.dot(gated, wq[...], preferred_element_type=F32)
    k_part = jnp.dot(gated, wk[...], preferred_element_type=F32)
    v_part = jnp.dot(gated, wv[...], preferred_element_type=F32)
    part = jnp.concatenate([q_part, k_part, v_part], axis=1)
    square = jnp.sum(rows * rows, axis=1, keepdims=True)
    square_hi = square.astype(BF16).astype(F32)
    square_tile = jnp.where(iota((ROWS, HEAD), 1) == 0, square_hi, square - square_hi)
    for j in range(8):
        for g in range(4):
            tile = jnp.concatenate(
                [
                    part[g * 8 : g * 8 + 8, j * HEAD : (j + 1) * HEAD],
                    square_tile[g * 8 : g * 8 + 8, :],
                ],
                axis=0,
            )
            qkv_out[j * 4 + g] = tile.astype(BF16)

    pl.semaphore_wait(barrier, CTX - 1 + TEN - 1)

    @pl.loop(0, CTX - 1)
    def _(i):
        p = peer_of(x, z, i)
        send(0, qkv_out.at[p], qkv_in.at[i], (p, t))

    leaves(0, qkv_in.at[pl.ds(0, CTX - 1)])

    qkv_in[CTX - 1] = qkv_out[c]
    wait(recv_sem.at[0], qkv_in.at[pl.ds(0, CTX - 1)])
    total = jnp.sum(qkv_in[...].astype(F32), axis=0)
    squares = total[8:16, 0:1] + total[8:16, 1:2]
    inv = lax.rsqrt(squares / WIDTH + EPS)
    mine = pl.multiple_of(c * 8, 8)
    qkv_all[pl.ds(mine, 8), :] = (total[0:8, :] * inv).astype(BF16).astype(F32)

    @pl.loop(0, CTX - 1)
    def _(i):
        tile = qkv_all.at[pl.ds(mine, 8)]
        send(1, tile, tile, (peer_of(x, z, i), t))

    leaves(1, qkv_all.at[pl.ds(0, 8 * (CTX - 1))])

    wait(recv_sem.at[1], qkv_all.at[pl.ds(0, 8 * (CTX - 1))])

    loads[13].wait()
    loads[6].wait()
    loads[7].wait()
    lane = iota((8, 2 * POS), 1)
    own_head = (lane % 2) == (iota((8, 2 * POS), 0) // 4)
    position = c * POS + lane // 2

    @pl.loop(0, 2)
    def _(n):
        homes = [ring_peer(x, 2 * n + m, 4) for m in range(2)]
        requests = [home * 4 + m for home in homes for m in range(4)]
        queries = [qkv_all[pl.ds(r, 8, stride=16), :].astype(BF16) for r in requests]
        scores = [nt_dot(q, kc[r]) * SCALE for q, r in zip(queries, requests)]
        live = [own_head & (position < lengths[r]) for r in requests]
        peaks = [
            jnp.max(jnp.where(l, s, MASKED), axis=1, keepdims=True) for s, l in zip(scores, live)
        ]
        weights = [
            jnp.where(l, jnp.exp(s - m), 0.0) for s, l, m in zip(scores, live, peaks)
        ]
        sums = [jnp.sum(w, axis=1, keepdims=True) for w in weights]
        mixtures = [
            jnp.dot(w.astype(BF16), vc[r], preferred_element_type=F32)
            for w, r in zip(weights, requests)
        ]
        for r, m, total, mixture in zip(requests, peaks, sums, mixtures):
            stats = jnp.where(iota((8, HEAD), 1) < 64, m, total)
            mix_out[2 * r] = jnp.concatenate([mixture[0:4], stats[0:4]], axis=0)
            mix_out[2 * r + 1] = jnp.concatenate([mixture[4:8], stats[4:8]], axis=0)

        @pl.loop(0, 16)
        def _(i):
            p = ring_peer(x, 2 * n + i % 2, 4) * 8 + ring_peer(z, i // 2)

            @pl.when(p != c)
            def _():
                send(2, mix_out.at[p], mix_in.at[16 * n + i], (p, t))

    leaves(2, mix_in.at[pl.ds(0, CTX - 1)])

    mix_in[CTX - 1] = mix_out[c]
    request, kv = c // 2, c % 2

    def new_row(j, s):
        return qkv_all[pl.ds(j * 32 + s * 16 + request, 1), :]

    query = jnp.concatenate([new_row(2 * kv + m // 2, m % 2) for m in range(4)], axis=0)
    own = [
        jnp.sum(query * new_row(4 + kv, s), axis=1, keepdims=True) * SCALE for s in range(2)
    ]
    second = (iota((4, 1), 0) % 2) == 1
    own[1] = jnp.where(second, own[1], MASKED)
    wait(recv_sem.at[2], mix_in.at[pl.ds(0, CTX - 1)])
    mixed = mix_in[:, 0:4, :]
    peaks = mix_in[:, 4:8, 0:1]
    sums = mix_in[:, 4:8, 64:65]
    highest = jnp.maximum(jnp.max(peaks, axis=0), jnp.maximum(own[0], own[1]))
    rescale = jnp.exp(peaks - highest[None])
    denominator = jnp.sum(rescale * sums, axis=0)
    numerator = jnp.sum(rescale * mixed, axis=0)
    own_weight = [jnp.exp(own[0] - highest), jnp.where(second, jnp.exp(own[1] - highest), 0.0)]
    for s in range(2):
        denominator = denominator + own_weight[s]
        numerator = numerator + own_weight[s] * new_row(6 + kv, s)
    attended = (numerator / denominator).astype(BF16).astype(F32)
    att_all[pl.ds(mine, 8), :] = jnp.concatenate([attended, attended], axis=0)

    @pl.loop(0, CTX - 1)
    def _(i):
        tile = att_all.at[pl.ds(mine, 8)]
        send(3, tile, tile, (peer_of(x, z, i), t))

    leaves(3, att_all.at[pl.ds(0, 8 * (CTX - 1))])

    loads[8].wait()
    wait(recv_sem.at[3], att_all.at[pl.ds(0, 8 * (CTX - 1))])

    att = jnp.concatenate(
        [
            jnp.concatenate(
                [
                    att_all[pl.ds((j // 2) * 8 + (j % 2) * 2 + s, REQS, stride=16), :]
                    for s in range(2)
                ],
                axis=0,
            )
            for j in range(4)
        ],
        axis=1,
    ).astype(BF16)
    pad = jnp.zeros((ROWS, 2 * HEAD - COLS), F32)

    def over_tensor(phase, value, slots):
        proj_out[phase - 4] = jnp.concatenate([value, pad], axis=1).astype(BF16)

        @pl.loop(0, TEN - 1)
        def _(i):
            send(phase, proj_out.at[phase - 4], slots.at[t], (c, ring_peer(t, i)))

        leaves(phase, slots.at[pl.ds(0, TEN - 1)])

        slots[t] = proj_out[phase - 4]
        wait(recv_sem.at[phase], slots.at[pl.ds(0, TEN - 1)])
        return jnp.sum(slots[...].astype(F32), axis=0)[:, 0:COLS]

    residual = rows + over_tensor(4, nt_dot(att, wo[...]), proj_in)

    square = jnp.sum(residual * residual, axis=1, keepdims=True)
    diagonal = iota((ROWS, HEAD), 0) == iota((ROWS, HEAD), 1)
    sq_out[...] = jnp.sum(jnp.where(diagonal, square, 0.0), axis=0, keepdims=True)

    sq_in[CTX - 1] = sq_out[...]
    loads[12].wait()
    loads[14].wait()
    ffn_gated = (residual * gain2[...].astype(F32)[None, :]).astype(BF16)
    loads[9].wait()
    loads[10].wait()

    def partial(k, tiles):
        columns = pl.ds(pl.multiple_of(k * 256, 256), HEAD * tiles)
        gate = jnp.dot(ffn_gated, wg[:, columns], preferred_element_type=F32).astype(BF16)
        up = jnp.dot(ffn_gated, wu[:, columns], preferred_element_type=F32).astype(BF16)
        for a in range(2 * tiles):
            rows_of, columns_of = slice(a % 2 * 16, a % 2 * 16 + 16), slice(a // 2 * HEAD, a // 2 * HEAD + HEAD)
            gu_out[4 * k + a, 0:16, :] = gate[rows_of, columns_of]
            gu_out[4 * k + a, 16:32, :] = up[rows_of, columns_of]

    def along_x(n, k, i):
        a = ring_peer(x, i, 4)
        pltpu.make_async_remote_copy(
            src_ref=gu_out.at[4 * k + a],
            dst_ref=gx_in.at[n, i],
            send_sem=gx_send.at[n],
            recv_sem=gx_recv.at[n],
            device_id=(a * 8 + z, t),
            device_id_type=MESH,
        ).start()

    for n in range(3):
        partial(8 + n, 2 if n < 2 else 1)
        for i in range(3):
            if n < 2:
                along_x(n, 8 + n, i)
            else:

                @pl.when(ring_peer(x, i, 4) < 2)
                def _():
                    along_x(2, 10, i)

    @pl.loop(0, 8)
    def _(n):
        k = ring_peer(z, n)
        partial(k, 2)
        for i in range(3):
            along_x(3 + n, k, i)

    @pl.loop(0, CTX - 1)
    def _(i):
        send(6, sq_out, sq_in.at[i], (peer_of(x, z, i), t))

    leaves(6, sq_in.at[pl.ds(0, CTX - 1)])

    def x_sum(n, k):
        wait(gx_recv.at[n], gx_in.at[n])
        total = gu_out[4 * k + x].astype(F32)
        for i in range(3):
            total = total + gx_in[n, i].astype(F32)
        return total.astype(BF16)

    for n in range(3):
        here = (x < 4) if n < 2 else (x < 2)

        @pl.when(here & (z == n))
        def _():
            gz_in2[z] = x_sum(n, 8 + n)

        @pl.when(here & (z != n))
        def _():
            gz_out[n] = x_sum(n, 8 + n)
            pltpu.make_async_remote_copy(
                src_ref=gz_out.at[n],
                dst_ref=gz_in2.at[z],
                send_sem=gz_send.at[n],
                recv_sem=recv_sem.at[8],
                device_id=(x * 8 + n, t),
                device_id_type=MESH,
            ).start()

    @pl.loop(0, 7)
    def _(n):
        k = ring_peer(z, n)
        gz_out[3 + n] = x_sum(3 + n, k)
        send(7, gz_out.at[3 + n], gz_in.at[n], (x * 8 + k, t))

    gz_in[7] = x_sum(10, z)
    leaves(7, gz_in.at[pl.ds(0, 7)])

    def sent_extra():
        for n in range(3):
            if n < 2:
                wait(gx_send.at[n], gx_in.at[n])
            else:

                @pl.when(x < 2)
                def _():
                    wait(gx_send.at[n], gx_in.at[n, pl.ds(0, 1)])

                @pl.when(x >= 2)
                def _():
                    wait(gx_send.at[n], gx_in.at[n, pl.ds(0, 2)])

            @pl.when(((x < 4) if n < 2 else (x < 2)) & (z != n))
            def _():
                wait(gz_send.at[n], gz_out.at[n])

        @pl.loop(3, 11)
        def _(n):
            wait(gx_send.at[n], gx_in.at[n])

    left.append(sent_extra)
    extra = (z < 2) | ((z == 2) & (x < 2))

    wait(recv_sem.at[6], sq_in.at[pl.ds(0, CTX - 1)])
    squares = jnp.sum(sq_in[...], axis=0)
    step_rows = iota((REQS, HEAD), 1) == iota((REQS, HEAD), 0) + REQS * (x % 2)
    squares = jnp.sum(jnp.where(step_rows, squares, 0.0), axis=1, keepdims=True)
    ffn_inv = lax.rsqrt(squares / WIDTH + EPS)
    levels = jnp.zeros((REQS, 1), jnp.int32)
    for r in range(REQS):
        levels = jnp.where(iota((REQS, 1), 0) == r, granularity[r], levels)
    active = levels > t

    def hidden_of(slots):
        both = jnp.sum(slots[...].astype(F32), axis=0)
        gate = both[0:16] * ffn_inv
        up = both[16:32] * ffn_inv
        act = 0.5 * gate * (1.0 + jnp.tanh(GELU * (gate + 0.044715 * (gate * gate * gate))))
        return jnp.where(active, act * up, 0.0).astype(BF16)

    def share(phase, unit):
        part_of = hid_all.at[pl.ds(pl.multiple_of(unit * 16, 16), 16)]

        @pl.loop(0, CTX - 1)
        def _(i):
            send(phase, part_of, part_of, (peer_of(x, z, i), t))

    def unit_rows(unit):
        return pl.ds(pl.multiple_of(unit * 16, 16), 16)

    @pl.when(extra)
    def _():
        wait(recv_sem.at[8], gz_in2.at[pl.ds(0, 7)])
        hid_all[unit_rows(32 + 4 * z + x), :] = hidden_of(gz_in2)
        share(10, 32 + 4 * z + x)

    wait(recv_sem.at[7], gz_in.at[pl.ds(0, 7)])
    hid_all[unit_rows(4 * z + x), :] = hidden_of(gz_in)
    share(9, 4 * z + x)
    leaves(9, hid_all.at[pl.ds(0, 16 * (CTX - 1))])

    def second_left():
        @pl.when(extra)
        def _():
            wait(send_sem.at[10], hid_all.at[pl.ds(0, 16 * (CTX - 1))])

    left.append(second_left)

    loads[11].wait()

    @pl.when(extra)
    def _():
        wait(recv_sem.at[10], hid_all.at[pl.ds(0, 16 * (EXTRA - 1))])

    @pl.when(jnp.logical_not(extra))
    def _():
        wait(recv_sem.at[10], hid_all.at[pl.ds(0, 16 * EXTRA)])

    wait(recv_sem.at[9], hid_all.at[pl.ds(0, 16 * (CTX - 1))])
    hidden = jnp.concatenate(
        [hid_all[i * ROWS : (i + 1) * ROWS, :] for i in range(TILES)], axis=1
    )
    output = residual + over_tensor(5, nt_dot(hidden, wd[...]), down_in)
    output = output.astype(BF16)
    o1_ref[...] = output[0:REQS]
    o2_ref[...] = output[REQS:ROWS]

    for sent in left:
        sent()


def per_device(
    first_input,
    second_input,
    attn_gain,
    query_weight,
    key_weight,
    value_weight,
    out_weight,
    ffn_gain,
    gate_weight,
    up_weight,
    down_weight,
    key_cache,
    value_cache,
    lengths,
    granularity,
):
    hbm = pl.BlockSpec(memory_space=pltpu.HBM)
    vmem = pl.BlockSpec(memory_space=pltpu.VMEM)
    V = pltpu.VMEM
    return pl.pallas_call(
        kernel,
        out_shape=(
            jax.ShapeDtypeStruct((REQS, COLS), BF16),
            jax.ShapeDtypeStruct((REQS, COLS), BF16),
        ),
        in_specs=[hbm] * 15,
        out_specs=(vmem, vmem),
        scratch_shapes=[
            pltpu.SMEM((REQS,), jnp.int32),
            pltpu.SMEM((REQS,), jnp.int32),
            V((REQS, COLS), BF16),
            V((REQS, COLS), BF16),
            V((COLS,), BF16),
            V((COLS,), BF16),
            V((COLS, 512), BF16),
            V((COLS, 256), BF16),
            V((COLS, 256), BF16),
            V((COLS, 512), BF16),
            V((COLS, 2688), BF16),
            V((COLS, 2688), BF16),
            V((COLS, 2688), BF16),
            V((REQS, 2 * POS, HEAD), BF16),
            V((REQS, 2 * POS, HEAD), BF16),
            V((CTX, 16, HEAD), BF16),
            V((CTX, 16, HEAD), BF16),
            V((CTX * 8, HEAD), F32),
            V((CTX, 8, HEAD), F32),
            V((CTX, 8, HEAD), F32),
            V((CTX * 8, HEAD), F32),
            V((2, ROWS, 2 * HEAD), BF16),
            V((TEN, ROWS, 2 * HEAD), BF16),
            V((1, HEAD), F32),
            V((CTX, 1, HEAD), F32),
            V((2 * TILES, 32, HEAD), BF16),
            V((11, 3, 32, HEAD), BF16),
            V((10, 32, HEAD), BF16),
            V((8, 32, HEAD), BF16),
            V((8, 32, HEAD), BF16),
            V((TILES * ROWS, HEAD), BF16),
            V((TEN, ROWS, 2 * HEAD), BF16),
            pltpu.SemaphoreType.DMA((15,)),
            pltpu.SemaphoreType.DMA((11,)),
            pltpu.SemaphoreType.DMA((11,)),
            pltpu.SemaphoreType.DMA((11,)),
            pltpu.SemaphoreType.DMA((11,)),
            pltpu.SemaphoreType.DMA((3,)),
        ],
        compiler_params=pltpu.CompilerParams(
            collective_id=0, has_side_effects=True, vmem_limit_bytes=56 * 2**20
        ),
    )(
        lengths,
        granularity,
        first_input,
        second_input,
        attn_gain,
        ffn_gain,
        query_weight,
        key_weight,
        value_weight,
        out_weight.T,
        gate_weight,
        up_weight,
        down_weight.T,
        key_cache.reshape(REQS, 2 * POS, HEAD),
        value_cache.reshape(REQS, 2 * POS, HEAD),
    )


def solution(mesh):
    return jax.shard_map(
        per_device,
        mesh=mesh,
        in_specs=(
            P(None, "context"),
            P(None, "context"),
            P("context"),
            P("context", "tensor"),
            P("context", "tensor"),
            P("context", "tensor"),
            P("tensor", "context"),
            P("context"),
            P("context", "tensor"),
            P("context", "tensor"),
            P("tensor", "context"),
            P(None, "context", "tensor", None),
            P(None, "context", "tensor", None),
            P(),
            P(),
        ),
        out_specs=(P(None, "context"), P(None, "context")),
        check_vma=False,
    )
```

```python
import math

import jax
import jax.numpy as jnp
from jax import lax
from jax.experimental import pallas as pl
from jax.experimental.pallas import tpu as pltpu
from jax.sharding import PartitionSpec as P

EPS = 1e-06
MASKED = -1e30
WIDTH = 5376
COLS = 168
HEAD = 128
CTX = 32
TEN = 8
REQS = 16
ROWS = 32
POS = 512
TILES = 21
EXTRA = 10
SCALE = HEAD**-0.5
GELU = math.sqrt(2.0 / math.pi)
MESH = pl.DeviceIdType.MESH
F32 = jnp.float32
BF16 = jnp.bfloat16


def iota(shape, dim):
    return lax.broadcasted_iota(jnp.int32, shape, dim)


def ring_peer(me, i, size=8):
    return lax.rem(me + size // 2 + ((i + 1) // 2) * (1 - 2 * (i % 2)), size)


def peer_of(x, z, i):
    return ring_peer(x, i % 4, 4) * 8 + ring_peer(z, i // 4)


def nt_dot(a, b):
    return lax.dot_general(a, b, (((1,), (1,)), ((), ())), preferred_element_type=F32)


def kernel(
    lengths_hbm,
    granularity_hbm,
    x1_hbm,
    x2_hbm,
    gain1_hbm,
    gain2_hbm,
    wq_hbm,
    wk_hbm,
    wv_hbm,
    wo_hbm,
    wg_hbm,
    wu_hbm,
    wd_hbm,
    kc_hbm,
    vc_hbm,
    o1_ref,
    o2_ref,
    lengths,
    granularity,
    x1,
    x2,
    gain1,
    gain2,
    wq,
    wk,
    wv,
    wo,
    wg,
    wu,
    wd,
    kc,
    vc,
    q_out,
    qx_in,
    qz_in,
    kv_out,
    kvx_in,
    kvz_in,
    new_sq,
    sqx_in,
    sqz_in,
    qkv_all,
    mix_out,
    mix_in,
    att_all,
    proj_out,
    proj_in,
    sq_out,
    sq_in,
    gu_out,
    gx_in,
    gz_out,
    gz_in,
    gz_in2,
    hid_all,
    down_in,
    local_sem,
    send_sem,
    recv_sem,
    gx_send,
    gx_recv,
    gz_send,
):
    c = lax.axis_index("context")
    t = lax.axis_index("tensor")
    x, z = c // 8, c % 8

    def local(i, src, dst):
        return pltpu.make_async_copy(src, dst, local_sem.at[i])

    loads = [
        local(0, x1_hbm, x1),
        local(1, x2_hbm, x2),
        local(2, gain1_hbm, gain1),
        local(3, wq_hbm, wq),
        local(4, wk_hbm, wk),
        local(5, wv_hbm, wv),
        local(6, kc_hbm, kc),
        local(7, vc_hbm, vc),
        local(8, wo_hbm, wo),
        local(9, wg_hbm, wg),
        local(10, wu_hbm, wu),
        local(11, wd_hbm, wd),
        local(12, gain2_hbm, gain2),
        local(13, lengths_hbm, lengths),
        local(14, granularity_hbm, granularity),
    ]
    barrier = pltpu.get_barrier_semaphore()

    @pl.loop(0, 7)
    def _(i):
        pl.semaphore_signal(
            barrier, inc=1, device_id=(x * 8 + ring_peer(z, i), t), device_id_type=MESH
        )

    @pl.loop(0, 3)
    def _(i):
        pl.semaphore_signal(
            barrier, inc=1, device_id=(ring_peer(x, i, 4) * 8 + z, t), device_id_type=MESH
        )

    @pl.loop(0, TEN - 1)
    def _(i):
        pl.semaphore_signal(
            barrier, inc=1, device_id=(c, ring_peer(t, i)), device_id_type=MESH
        )

    for load in loads:
        load.start()

    def send(phase, src, dst, peer):
        pltpu.make_async_remote_copy(
            src_ref=src,
            dst_ref=dst,
            send_sem=send_sem.at[phase],
            recv_sem=recv_sem.at[phase],
            device_id=peer,
            device_id_type=MESH,
        ).start()

    def wait(sem, ref):
        pltpu.make_async_copy(ref, ref, sem).wait()

    left = []

    def leaves(phase, ref):
        left.append(lambda: wait(send_sem.at[phase], ref))

    for i in range(6):
        loads[i].wait()
    rows = jnp.concatenate([x1[...], x2[...]], axis=0).astype(F32)
    gated = (rows * gain1[...].astype(F32)[None, :]).astype(BF16)
    q_part = jnp.dot(gated, wq[...], preferred_element_type=F32)
    k_part = jnp.dot(gated, wk[...], preferred_element_type=F32)
    v_part = jnp.dot(gated, wv[...], preferred_element_type=F32)
    q_out[0] = q_part[0:REQS].astype(BF16)
    q_out[1] = q_part[REQS:ROWS].astype(BF16)
    kv_out[0] = jnp.concatenate([k_part, v_part], axis=1).astype(BF16)
    diagonal = iota((ROWS, HEAD), 0) == iota((ROWS, HEAD), 1)

    def as_row(column):
        return jnp.sum(jnp.where(diagonal, column, 0.0), axis=0, keepdims=True)

    def as_column(row):
        return jnp.sum(jnp.where(diagonal, row, 0.0), axis=1, keepdims=True)

    new_sq[0] = as_row(jnp.sum(rows * rows, axis=1, keepdims=True))

    pl.semaphore_wait(barrier, 7 + 3 + TEN - 1)

    def along_x_all(phase, src, slots):
        @pl.loop(0, 3)
        def _(i):
            send(phase, src, slots.at[i], (ring_peer(x, i, 4) * 8 + z, t))

        leaves(phase, slots)

    def along_z_all(phase, src, slots):
        @pl.loop(0, 7)
        def _(i):
            send(phase, src, slots.at[i], (x * 8 + ring_peer(z, i), t))

        leaves(phase, slots)

    def sum_of(phase, own, slots):
        wait(recv_sem.at[phase], slots)
        return own[...].astype(F32) + jnp.sum(slots[...].astype(F32), axis=0)

    along_z_all(1, q_out.at[1], qz_in.at[1])
    along_x_all(0, q_out.at[0], qx_in.at[0])
    along_x_all(11, new_sq.at[0], sqx_in)
    along_x_all(12, kv_out.at[0], kvx_in)
    new_sq[1] = sum_of(11, new_sq.at[0], sqx_in)
    q_out[2] = sum_of(0, q_out.at[0], qx_in.at[0]).astype(BF16)
    along_z_all(13, q_out.at[2], qz_in.at[0])
    along_z_all(14, new_sq.at[1], sqz_in)
    q_out[3] = sum_of(1, q_out.at[1], qz_in.at[1]).astype(BF16)
    along_x_all(15, q_out.at[3], qx_in.at[1])
    kv_out[1] = sum_of(12, kv_out.at[0], kvx_in).astype(BF16)
    along_z_all(16, kv_out.at[1], kvz_in)
    squares = as_column(sum_of(14, new_sq.at[1], sqz_in))
    inv = lax.rsqrt(squares / WIDTH + EPS)
    totals = [
        sum_of(13, q_out.at[2], qz_in.at[0]),
        sum_of(15, q_out.at[3], qx_in.at[1]),
    ]
    for s in range(2):
        query = (totals[s] * inv[s * REQS : s * REQS + REQS]).astype(BF16).astype(F32)
        for j in range(4):
            start = (2 * j + s) * REQS
            qkv_all[start : start + REQS, :] = query[:, j * HEAD : (j + 1) * HEAD]

    loads[13].wait()
    loads[6].wait()
    loads[7].wait()
    lane = iota((8, 2 * POS), 1)
    own_head = (lane % 2) == (iota((8, 2 * POS), 0) // 4)
    position = c * POS + lane // 2

    @pl.loop(0, 2)
    def _(n):
        homes = [ring_peer(x, 2 * n + m, 4) for m in range(2)]
        requests = [home * 4 + m for home in homes for m in range(4)]
        queries = [qkv_all[pl.ds(r, 8, stride=16), :].astype(BF16) for r in requests]
        scores = [nt_dot(q, kc[r]) * SCALE for q, r in zip(queries, requests)]
        live = [own_head & (position < lengths[r]) for r in requests]
        peaks = [
            jnp.max(jnp.where(l, s, MASKED), axis=1, keepdims=True) for s, l in zip(scores, live)
        ]
        weights = [
            jnp.where(l, jnp.exp(s - m), 0.0) for s, l, m in zip(scores, live, peaks)
        ]
        sums = [jnp.sum(w, axis=1, keepdims=True) for w in weights]
        mixtures = [
            jnp.dot(w.astype(BF16), vc[r], preferred_element_type=F32)
            for w, r in zip(weights, requests)
        ]
        for r, m, total, mixture in zip(requests, peaks, sums, mixtures):
            stats = jnp.where(iota((8, HEAD), 1) < 64, m, total)
            mix_out[2 * r] = jnp.concatenate([mixture[0:4], stats[0:4]], axis=0)
            mix_out[2 * r + 1] = jnp.concatenate([mixture[4:8], stats[4:8]], axis=0)

        @pl.loop(0, 16)
        def _(i):
            p = ring_peer(x, 2 * n + i % 2, 4) * 8 + ring_peer(z, i // 2)

            @pl.when(p != c)
            def _():
                send(2, mix_out.at[p], mix_in.at[16 * n + i], (p, t))

    leaves(2, mix_in.at[pl.ds(0, CTX - 1)])

    mix_in[CTX - 1] = mix_out[c]
    request, kv = c // 2, c % 2
    mine = pl.multiple_of(c * 8, 8)
    new = (sum_of(16, kv_out.at[1], kvz_in) * inv).astype(BF16).astype(F32)
    for j in range(4):
        qkv_all[(4 + j) * ROWS : (5 + j) * ROWS, :] = new[:, j * HEAD : (j + 1) * HEAD]

    def new_row(j, s):
        return qkv_all[pl.ds(j * 32 + s * 16 + request, 1), :]

    query = jnp.concatenate([new_row(2 * kv + m // 2, m % 2) for m in range(4)], axis=0)
    own = [
        jnp.sum(query * new_row(4 + kv, s), axis=1, keepdims=True) * SCALE for s in range(2)
    ]
    second = (iota((4, 1), 0) % 2) == 1
    own[1] = jnp.where(second, own[1], MASKED)
    wait(recv_sem.at[2], mix_in.at[pl.ds(0, CTX - 1)])
    mixed = mix_in[:, 0:4, :]
    peaks = mix_in[:, 4:8, 0:1]
    sums = mix_in[:, 4:8, 64:65]
    highest = jnp.maximum(jnp.max(peaks, axis=0), jnp.maximum(own[0], own[1]))
    rescale = jnp.exp(peaks - highest[None])
    denominator = jnp.sum(rescale * sums, axis=0)
    numerator = jnp.sum(rescale * mixed, axis=0)
    own_weight = [jnp.exp(own[0] - highest), jnp.where(second, jnp.exp(own[1] - highest), 0.0)]
    for s in range(2):
        denominator = denominator + own_weight[s]
        numerator = numerator + own_weight[s] * new_row(6 + kv, s)
    attended = (numerator / denominator).astype(BF16).astype(F32)
    att_all[pl.ds(mine, 8), :] = jnp.concatenate([attended, attended], axis=0)

    @pl.loop(0, CTX - 1)
    def _(i):
        tile = att_all.at[pl.ds(mine, 8)]
        send(3, tile, tile, (peer_of(x, z, i), t))

    leaves(3, att_all.at[pl.ds(0, 8 * (CTX - 1))])

    loads[8].wait()
    wait(recv_sem.at[3], att_all.at[pl.ds(0, 8 * (CTX - 1))])

    att = jnp.concatenate(
        [
            jnp.concatenate(
                [
                    att_all[pl.ds((j // 2) * 8 + (j % 2) * 2 + s, REQS, stride=16), :]
                    for s in range(2)
                ],
                axis=0,
            )
            for j in range(4)
        ],
        axis=1,
    ).astype(BF16)
    pad = jnp.zeros((ROWS, 2 * HEAD - COLS), F32)

    def over_tensor(phase, value, slots):
        proj_out[phase - 4] = jnp.concatenate([value, pad], axis=1).astype(BF16)

        @pl.loop(0, TEN - 1)
        def _(i):
            send(phase, proj_out.at[phase - 4], slots.at[t], (c, ring_peer(t, i)))

        leaves(phase, slots.at[pl.ds(0, TEN - 1)])

        slots[t] = proj_out[phase - 4]
        wait(recv_sem.at[phase], slots.at[pl.ds(0, TEN - 1)])
        return jnp.sum(slots[...].astype(F32), axis=0)[:, 0:COLS]

    residual = rows + over_tensor(4, nt_dot(att, wo[...]), proj_in)

    square = jnp.sum(residual * residual, axis=1, keepdims=True)
    sq_out[...] = as_row(square)

    sq_in[CTX - 1] = sq_out[...]
    loads[12].wait()
    loads[14].wait()
    ffn_gated = (residual * gain2[...].astype(F32)[None, :]).astype(BF16)
    loads[9].wait()
    loads[10].wait()

    def partial(k, tiles):
        columns = pl.ds(pl.multiple_of(k * 256, 256), HEAD * tiles)
        gate = jnp.dot(ffn_gated, wg[:, columns], preferred_element_type=F32).astype(BF16)
        up = jnp.dot(ffn_gated, wu[:, columns], preferred_element_type=F32).astype(BF16)
        for a in range(2 * tiles):
            rows_of, columns_of = slice(a % 2 * 16, a % 2 * 16 + 16), slice(a // 2 * HEAD, a // 2 * HEAD + HEAD)
            gu_out[4 * k + a, 0:16, :] = gate[rows_of, columns_of]
            gu_out[4 * k + a, 16:32, :] = up[rows_of, columns_of]

    def along_x(n, k, i):
        a = ring_peer(x, i, 4)
        pltpu.make_async_remote_copy(
            src_ref=gu_out.at[4 * k + a],
            dst_ref=gx_in.at[n, i],
            send_sem=gx_send.at[n],
            recv_sem=gx_recv.at[n],
            device_id=(a * 8 + z, t),
            device_id_type=MESH,
        ).start()

    for n in range(3):
        partial(8 + n, 2 if n < 2 else 1)
        for i in range(3):
            if n < 2:
                along_x(n, 8 + n, i)
            else:

                @pl.when(ring_peer(x, i, 4) < 2)
                def _():
                    along_x(2, 10, i)

    @pl.loop(0, 8)
    def _(n):
        k = ring_peer(z, n)
        partial(k, 2)
        for i in range(3):
            along_x(3 + n, k, i)

    @pl.loop(0, CTX - 1)
    def _(i):
        send(6, sq_out, sq_in.at[i], (peer_of(x, z, i), t))

    leaves(6, sq_in.at[pl.ds(0, CTX - 1)])

    def x_sum(n, k):
        wait(gx_recv.at[n], gx_in.at[n])
        total = gu_out[4 * k + x].astype(F32)
        for i in range(3):
            total = total + gx_in[n, i].astype(F32)
        return total.astype(BF16)

    for n in range(3):
        here = (x < 4) if n < 2 else (x < 2)

        @pl.when(here & (z == n))
        def _():
            gz_in2[z] = x_sum(n, 8 + n)

        @pl.when(here & (z != n))
        def _():
            gz_out[n] = x_sum(n, 8 + n)
            pltpu.make_async_remote_copy(
                src_ref=gz_out.at[n],
                dst_ref=gz_in2.at[z],
                send_sem=gz_send.at[n],
                recv_sem=recv_sem.at[8],
                device_id=(x * 8 + n, t),
                device_id_type=MESH,
            ).start()

    @pl.loop(0, 7)
    def _(n):
        k = ring_peer(z, n)
        gz_out[3 + n] = x_sum(3 + n, k)
        send(7, gz_out.at[3 + n], gz_in.at[n], (x * 8 + k, t))

    gz_in[7] = x_sum(10, z)
    leaves(7, gz_in.at[pl.ds(0, 7)])

    def sent_extra():
        for n in range(3):
            if n < 2:
                wait(gx_send.at[n], gx_in.at[n])
            else:

                @pl.when(x < 2)
                def _():
                    wait(gx_send.at[n], gx_in.at[n, pl.ds(0, 1)])

                @pl.when(x >= 2)
                def _():
                    wait(gx_send.at[n], gx_in.at[n, pl.ds(0, 2)])

            @pl.when(((x < 4) if n < 2 else (x < 2)) & (z != n))
            def _():
                wait(gz_send.at[n], gz_out.at[n])

        @pl.loop(3, 11)
        def _(n):
            wait(gx_send.at[n], gx_in.at[n])

    left.append(sent_extra)
    extra = (z < 2) | ((z == 2) & (x < 2))

    wait(recv_sem.at[6], sq_in.at[pl.ds(0, CTX - 1)])
    squares = jnp.sum(sq_in[...], axis=0)
    step_rows = iota((REQS, HEAD), 1) == iota((REQS, HEAD), 0) + REQS * (x % 2)
    squares = jnp.sum(jnp.where(step_rows, squares, 0.0), axis=1, keepdims=True)
    ffn_inv = lax.rsqrt(squares / WIDTH + EPS)
    levels = jnp.zeros((REQS, 1), jnp.int32)
    for r in range(REQS):
        levels = jnp.where(iota((REQS, 1), 0) == r, granularity[r], levels)
    active = levels > t

    def hidden_of(slots):
        both = jnp.sum(slots[...].astype(F32), axis=0)
        gate = both[0:16] * ffn_inv
        up = both[16:32] * ffn_inv
        act = 0.5 * gate * (1.0 + jnp.tanh(GELU * (gate + 0.044715 * (gate * gate * gate))))
        return jnp.where(active, act * up, 0.0).astype(BF16)

    def share(phase, unit):
        part_of = hid_all.at[pl.ds(pl.multiple_of(unit * 16, 16), 16)]

        @pl.loop(0, CTX - 1)
        def _(i):
            send(phase, part_of, part_of, (peer_of(x, z, i), t))

    def unit_rows(unit):
        return pl.ds(pl.multiple_of(unit * 16, 16), 16)

    @pl.when(extra)
    def _():
        wait(recv_sem.at[8], gz_in2.at[pl.ds(0, 7)])
        hid_all[unit_rows(32 + 4 * z + x), :] = hidden_of(gz_in2)
        share(10, 32 + 4 * z + x)

    wait(recv_sem.at[7], gz_in.at[pl.ds(0, 7)])
    hid_all[unit_rows(4 * z + x), :] = hidden_of(gz_in)
    share(9, 4 * z + x)
    leaves(9, hid_all.at[pl.ds(0, 16 * (CTX - 1))])

    def second_left():
        @pl.when(extra)
        def _():
            wait(send_sem.at[10], hid_all.at[pl.ds(0, 16 * (CTX - 1))])

    left.append(second_left)

    loads[11].wait()

    @pl.when(extra)
    def _():
        wait(recv_sem.at[10], hid_all.at[pl.ds(0, 16 * (EXTRA - 1))])

    @pl.when(jnp.logical_not(extra))
    def _():
        wait(recv_sem.at[10], hid_all.at[pl.ds(0, 16 * EXTRA)])

    wait(recv_sem.at[9], hid_all.at[pl.ds(0, 16 * (CTX - 1))])
    hidden = jnp.concatenate(
        [hid_all[i * ROWS : (i + 1) * ROWS, :] for i in range(TILES)], axis=1
    )
    output = residual + over_tensor(5, nt_dot(hidden, wd[...]), down_in)
    output = output.astype(BF16)
    o1_ref[...] = output[0:REQS]
    o2_ref[...] = output[REQS:ROWS]

    for sent in left:
        sent()


def per_device(
    first_input,
    second_input,
    attn_gain,
    query_weight,
    key_weight,
    value_weight,
    out_weight,
    ffn_gain,
    gate_weight,
    up_weight,
    down_weight,
    key_cache,
    value_cache,
    lengths,
    granularity,
):
    hbm = pl.BlockSpec(memory_space=pltpu.HBM)
    vmem = pl.BlockSpec(memory_space=pltpu.VMEM)
    V = pltpu.VMEM
    return pl.pallas_call(
        kernel,
        out_shape=(
            pltpu.VMEM((REQS, COLS), BF16),
            pltpu.VMEM((REQS, COLS), BF16),
        ),
        in_specs=[hbm] * 15,
        out_specs=(vmem, vmem),
        scratch_shapes=[
            pltpu.SMEM((REQS,), jnp.int32),
            pltpu.SMEM((REQS,), jnp.int32),
            V((REQS, COLS), BF16),
            V((REQS, COLS), BF16),
            V((COLS,), BF16),
            V((COLS,), BF16),
            V((COLS, 512), BF16),
            V((COLS, 256), BF16),
            V((COLS, 256), BF16),
            V((COLS, 512), BF16),
            V((COLS, 2688), BF16),
            V((COLS, 2688), BF16),
            V((COLS, 2688), BF16),
            V((REQS, 2 * POS, HEAD), BF16),
            V((REQS, 2 * POS, HEAD), BF16),
            V((4, REQS, 512), BF16),
            V((2, 3, REQS, 512), BF16),
            V((2, 7, REQS, 512), BF16),
            V((2, ROWS, 512), BF16),
            V((3, ROWS, 512), BF16),
            V((7, ROWS, 512), BF16),
            V((2, 1, HEAD), F32),
            V((3, 1, HEAD), F32),
            V((7, 1, HEAD), F32),
            V((CTX * 8, HEAD), F32),
            V((CTX, 8, HEAD), F32),
            V((CTX, 8, HEAD), F32),
            V((CTX * 8, HEAD), F32),
            V((2, ROWS, 2 * HEAD), BF16),
            V((TEN, ROWS, 2 * HEAD), BF16),
            V((1, HEAD), F32),
            V((CTX, 1, HEAD), F32),
            V((2 * TILES, 32, HEAD), BF16),
            V((11, 3, 32, HEAD), BF16),
            V((10, 32, HEAD), BF16),
            V((8, 32, HEAD), BF16),
            V((8, 32, HEAD), BF16),
            V((TILES * ROWS, HEAD), BF16),
            V((TEN, ROWS, 2 * HEAD), BF16),
            pltpu.SemaphoreType.DMA((15,)),
            pltpu.SemaphoreType.DMA((17,)),
            pltpu.SemaphoreType.DMA((17,)),
            pltpu.SemaphoreType.DMA((11,)),
            pltpu.SemaphoreType.DMA((11,)),
            pltpu.SemaphoreType.DMA((3,)),
        ],
        compiler_params=pltpu.CompilerParams(
            collective_id=0, has_side_effects=True, vmem_limit_bytes=56 * 2**20
        ),
    )(
        lengths,
        granularity,
        first_input,
        second_input,
        attn_gain,
        ffn_gain,
        query_weight,
        key_weight,
        value_weight,
        out_weight.T,
        gate_weight,
        up_weight,
        down_weight.T,
        key_cache.reshape(REQS, 2 * POS, HEAD),
        value_cache.reshape(REQS, 2 * POS, HEAD),
    )


def solution(mesh):
    return jax.shard_map(
        per_device,
        mesh=mesh,
        in_specs=(
            P(None, "context"),
            P(None, "context"),
            P("context"),
            P("context", "tensor"),
            P("context", "tensor"),
            P("context", "tensor"),
            P("tensor", "context"),
            P("context"),
            P("context", "tensor"),
            P("context", "tensor"),
            P("tensor", "context"),
            P(None, "context", "tensor", None),
            P(None, "context", "tensor", None),
            P(),
            P(),
        ),
        out_specs=(P(None, "context"), P(None, "context")),
        check_vma=False,
    )
```

```python
import math

import jax
import jax.numpy as jnp
from jax import lax
from jax.experimental import pallas as pl
from jax.experimental.pallas import tpu as pltpu
from jax.sharding import PartitionSpec as P

EPS = 1e-06
MASKED = -1e30
WIDTH = 5376
COLS = 168
HEAD = 128
CTX = 32
TEN = 8
REQS = 16
ROWS = 32
POS = 512
TILES = 21
EXTRA = 10
SCALE = HEAD**-0.5
GELU = math.sqrt(2.0 / math.pi)
MESH = pl.DeviceIdType.MESH
F32 = jnp.float32
BF16 = jnp.bfloat16


def iota(shape, dim):
    return lax.broadcasted_iota(jnp.int32, shape, dim)


def ring_peer(me, i, size=8):
    return lax.rem(me + size // 2 + ((i + 1) // 2) * (1 - 2 * (i % 2)), size)


def peer_of(x, z, i):
    return ring_peer(x, i % 4, 4) * 8 + ring_peer(z, i // 4)


NEAR = [
    (0, 0),
    (0, 1),
    (0, 7),
    (1, 0),
    (3, 0),
    (2, 0),
    (0, 2),
    (0, 6),
    (1, 1),
    (1, 7),
    (3, 1),
    (3, 7),
    (0, 3),
    (0, 5),
    (1, 2),
    (1, 6),
]


def hops(offset):
    return min(offset[0], 4 - offset[0]) + min(offset[1], 8 - offset[1])


def opposite(offset):
    return ((offset[0] + 2) % 4, (offset[1] + 4) % 8)


def far_first(offsets):
    return sorted(offsets, key=hops, reverse=True)


def nt_dot(a, b):
    return lax.dot_general(a, b, (((1,), (1,)), ((), ())), preferred_element_type=F32)


def kernel(
    lengths_hbm,
    granularity_hbm,
    x1_hbm,
    x2_hbm,
    gain1_hbm,
    gain2_hbm,
    wq_hbm,
    wk_hbm,
    wv_hbm,
    wo_hbm,
    wg_hbm,
    wu_hbm,
    wd_hbm,
    kc_hbm,
    vc_hbm,
    out_ref,
    lengths,
    granularity,
    x1,
    x2,
    gain1,
    gain2,
    wq,
    wk,
    wv,
    wo,
    wg,
    wu,
    wd,
    kc,
    vc,
    q_out,
    qx_in,
    qz_in,
    kv_out,
    kv_in,
    inv_rows,
    new_sq,
    sqx_in,
    sqz_in,
    qkv_all,
    mix_out,
    mix_in,
    att_all,
    proj_out,
    proj_in,
    sq_out,
    sqfx_in,
    sqfz_in,
    gu_out,
    gx_in,
    gz_out,
    gz_in,
    gz_in2,
    hid_all,
    down_in,
    local_sem,
    send_sem,
    recv_sem,
    gx_send,
    gx_recv,
    gz_send,
):
    c = lax.axis_index("context")
    t = lax.axis_index("tensor")
    x, z = c // 8, c % 8

    def local(i, src, dst):
        return pltpu.make_async_copy(src, dst, local_sem.at[i])

    loads = [
        local(0, x1_hbm, x1),
        local(1, x2_hbm, x2),
        local(2, gain1_hbm, gain1),
        local(3, wq_hbm, wq),
        local(4, wk_hbm, wk),
        local(5, wv_hbm, wv),
        local(6, kc_hbm, kc),
        local(7, vc_hbm, vc),
        local(8, wo_hbm, wo),
        local(9, wg_hbm, wg),
        local(10, wu_hbm, wu),
        local(11, wd_hbm, wd),
        local(12, gain2_hbm, gain2),
        local(13, lengths_hbm, lengths),
        local(14, granularity_hbm, granularity),
    ]
    barrier = pltpu.get_barrier_semaphore()

    @pl.loop(0, 7)
    def _(i):
        pl.semaphore_signal(
            barrier, inc=1, device_id=(x * 8 + ring_peer(z, i), t), device_id_type=MESH
        )

    @pl.loop(0, 3)
    def _(i):
        pl.semaphore_signal(
            barrier, inc=1, device_id=(ring_peer(x, i, 4) * 8 + z, t), device_id_type=MESH
        )

    for load in loads[0:6]:
        load.start()

    @pl.loop(0, TEN - 1)
    def _(i):
        pl.semaphore_signal(
            barrier, inc=1, device_id=(c, ring_peer(t, i)), device_id_type=MESH
        )

    for load in loads[6:]:
        load.start()

    def send(phase, src, dst, peer):
        pltpu.make_async_remote_copy(
            src_ref=src,
            dst_ref=dst,
            send_sem=send_sem.at[phase],
            recv_sem=recv_sem.at[phase],
            device_id=peer,
            device_id_type=MESH,
        ).start()

    def wait(sem, ref):
        pltpu.make_async_copy(ref, ref, sem).wait()

    left = []

    def leaves(phase, ref):
        left.append(lambda: wait(send_sem.at[phase], ref))

    for i in range(6):
        loads[i].wait()
    rows = jnp.concatenate([x1[...], x2[...]], axis=0).astype(F32)
    gated = (rows * gain1[...].astype(F32)[None, :]).astype(BF16)
    q_part = jnp.dot(gated, wq[...], preferred_element_type=F32)
    k_part = jnp.dot(gated, wk[...], preferred_element_type=F32)
    v_part = jnp.dot(gated, wv[...], preferred_element_type=F32)
    q_out[0] = q_part[0:REQS].astype(BF16)
    q_out[1] = q_part[REQS:ROWS].astype(BF16)
    diagonal = iota((ROWS, HEAD), 0) == iota((ROWS, HEAD), 1)

    def as_row(column):
        return jnp.sum(jnp.where(diagonal, column, 0.0), axis=0, keepdims=True)

    def as_column(row):
        return jnp.sum(jnp.where(diagonal, row, 0.0), axis=1, keepdims=True)

    new_sq[0] = as_row(jnp.sum(rows * rows, axis=1, keepdims=True))

    pl.semaphore_wait(barrier, 7 + 3 + TEN - 1)

    def along_x_all(phase, src, slots):
        @pl.loop(0, 3)
        def _(i):
            send(phase, src, slots.at[i], (ring_peer(x, i, 4) * 8 + z, t))

        leaves(phase, slots)

    def along_z_all(phase, src, slots):
        @pl.loop(0, 7)
        def _(i):
            send(phase, src, slots.at[i], (x * 8 + ring_peer(z, i), t))

        leaves(phase, slots)

    def sum_of(phase, own, slots):
        wait(recv_sem.at[phase], slots)
        return own[...].astype(F32) + jnp.sum(slots[...].astype(F32), axis=0)

    along_z_all(1, q_out.at[1], qz_in.at[1])
    along_x_all(0, q_out.at[0], qx_in.at[0])
    along_x_all(11, new_sq.at[0], sqx_in)
    kv_part = jnp.concatenate([k_part, v_part], axis=1)
    for s in range(2):
        for j in range(4):
            kv_out[pl.ds(4 * s + j, REQS, stride=8), :] = kv_part[
                s * REQS : s * REQS + REQS, j * HEAD : (j + 1) * HEAD
            ]
    new_sq[1] = sum_of(11, new_sq.at[0], sqx_in)
    q_out[2] = sum_of(0, q_out.at[0], qx_in.at[0]).astype(BF16)
    along_z_all(13, q_out.at[2], qz_in.at[0])
    along_z_all(14, new_sq.at[1], sqz_in)
    q_out[3] = sum_of(1, q_out.at[1], qz_in.at[1]).astype(BF16)
    along_x_all(15, q_out.at[3], qx_in.at[1])
    squares = as_column(sum_of(14, new_sq.at[1], sqz_in))
    inv = lax.rsqrt(squares / WIDTH + EPS)
    inv_rows[...] = jnp.broadcast_to(inv, (ROWS, HEAD))
    second_total = sum_of(15, q_out.at[3], qx_in.at[1])

    def place(offset):
        return lax.rem(x + offset[0], 4), lax.rem(z + offset[1], 8)

    def request_at(at):
        return (at[0] % 2) * 8 + lax.rem(at[1] + 4 * (at[0] // 2), 8)

    def request_rows(ref, r):
        return ref.at[pl.ds(pl.multiple_of(r * 8, 8), 8)]

    for offset in far_first(NEAR + [opposite(offset) for offset in NEAR]):
        if offset != (0, 0):
            a, b = place(offset)
            send(12, request_rows(kv_out, request_at((a, b))), kv_in.at[c], (a * 8 + b, t))

    leaves(12, kv_in.at[pl.ds(0, CTX - 1)])
    totals = [sum_of(13, q_out.at[2], qz_in.at[0]), second_total]
    for s in range(2):
        query = (totals[s] * inv[s * REQS : s * REQS + REQS]).astype(BF16).astype(F32)
        for j in range(4):
            start = (2 * j + s) * REQS
            qkv_all[start : start + REQS, :] = query[:, j * HEAD : (j + 1) * HEAD]

    loads[13].wait()
    loads[6].wait()
    loads[7].wait()
    lane = iota((8, 2 * POS), 1)
    own_head = (lane % 2) == (iota((8, 2 * POS), 0) // 4)
    position = c * POS + lane // 2

    lane = iota((8, HEAD), 1)
    for half in (NEAR[:8], NEAR[8:]):
        requests = [request_at(place(offset)) for offset in half]
        queries = [qkv_all[pl.ds(r, 8, stride=16), :].astype(BF16) for r in requests]
        scores = [nt_dot(q, kc[r]) * SCALE for q, r in zip(queries, requests)]
        live = [own_head & (position < lengths[r]) for r in requests]
        peaks = [
            jnp.max(jnp.where(l, s, MASKED), axis=1, keepdims=True) for s, l in zip(scores, live)
        ]
        weights = [
            jnp.where(l, jnp.exp(s - m), 0.0) for s, l, m in zip(scores, live, peaks)
        ]
        sums = [jnp.sum(w, axis=1, keepdims=True) for w in weights]
        mixtures = [
            jnp.dot(w.astype(BF16), vc[r], preferred_element_type=F32)
            for w, r in zip(weights, requests)
        ]
        for r, m, total, mixture in zip(requests, peaks, sums, mixtures):
            first = m.astype(BF16).astype(F32)
            second = (m - first).astype(BF16).astype(F32)
            total_first = total.astype(BF16).astype(F32)
            stats = jnp.where(lane == 3, total_first, total - total_first)
            stats = jnp.where(lane == 2, m - first - second, stats)
            stats = jnp.where(lane == 1, second, stats)
            stats = jnp.where(lane == 0, first, stats)
            stats = jnp.where(lane > 4, 0.0, stats)
            mix_out[r] = jnp.concatenate([mixture, stats], axis=0).astype(BF16)
        for offset in far_first(half + [opposite(offset) for offset in half]):
            if offset != (0, 0):
                a, b = place(offset)
                send(2, mix_out.at[request_at((a, b))], mix_in.at[c], (a * 8 + b, t))

    leaves(2, mix_in.at[pl.ds(0, CTX - 1)])

    request = request_at((x, z))
    mix_in[c] = mix_out[request]
    kv_in[c] = request_rows(kv_out, request)[...]
    query = qkv_all[pl.ds(request, 8, stride=16), :]
    first_head = iota((8, 1), 0) < 4
    second_step = (iota((8, 1), 0) % 2) == 1
    inv_step = [inv_rows[pl.ds(s * REQS + request, 1), :] for s in range(2)]
    wait(recv_sem.at[12], kv_in.at[pl.ds(0, CTX - 1)])
    new = jnp.sum(kv_in[...], axis=0) * jnp.where(first_head, inv_step[0], inv_step[1])
    new = new.astype(BF16).astype(F32)

    def new_rows(j, s):
        return jnp.where(first_head, new[4 * s + j : 4 * s + j + 1], new[4 * s + j + 1 : 4 * s + j + 2])

    own = [jnp.sum(query * new_rows(0, s), axis=1, keepdims=True) * SCALE for s in range(2)]
    own[1] = jnp.where(second_step, own[1], MASKED)
    new_values = [new_rows(2, s) for s in range(2)]
    wait(recv_sem.at[2], mix_in.at[pl.ds(0, CTX - 1)])
    mixed = mix_in[:, 0:8, :].astype(F32)
    stats = mix_in[:, 8:16, :].astype(F32)
    lane = iota((CTX, 8, HEAD), 2)
    peaks = jnp.sum(jnp.where(lane < 3, stats, 0.0), axis=2, keepdims=True)
    sums = jnp.sum(jnp.where(lane < 3, 0.0, stats), axis=2, keepdims=True)
    highest = jnp.maximum(jnp.max(peaks, axis=0), jnp.maximum(own[0], own[1]))
    rescale = jnp.exp(peaks - highest[None])
    denominator = jnp.sum(rescale * sums, axis=0)
    numerator = jnp.sum(rescale * mixed, axis=0)
    own_weight = [
        jnp.exp(own[0] - highest),
        jnp.where(second_step, jnp.exp(own[1] - highest), 0.0),
    ]
    for s in range(2):
        denominator = denominator + own_weight[s]
        numerator = numerator + own_weight[s] * new_values[s]
    mine = att_all.at[pl.ds(pl.multiple_of(request * 8, 8), 8)]
    mine[...] = (numerator / denominator).astype(BF16).astype(F32)
    for offset in far_first(NEAR):
        if offset != (0, 0):
            a, b = place(offset)
            send(3, mine, mine, (a * 8 + b, t))

    leaves(3, att_all.at[pl.ds(0, 8 * (REQS - 1))])
    loads[8].wait()
    wait(recv_sem.at[3], att_all.at[pl.ds(0, 8 * (REQS - 1))])

    att = jnp.concatenate(
        [
            jnp.concatenate(
                [
                    att_all[pl.ds(2 * j + s, REQS, stride=8), :]
                    for s in range(2)
                ],
                axis=0,
            )
            for j in range(4)
        ],
        axis=1,
    ).astype(BF16)
    pad = jnp.zeros((ROWS, 2 * HEAD - COLS), F32)

    def over_tensor(phase, value, slots):
        proj_out[phase - 4] = jnp.concatenate([value, pad], axis=1).astype(BF16)

        @pl.loop(0, TEN - 1)
        def _(i):
            send(phase, proj_out.at[phase - 4], slots.at[t], (c, ring_peer(t, i)))

        if phase == 5:
            while left:
                left.pop(0)()
        leaves(phase, slots.at[pl.ds(0, TEN - 1)])

        slots[t] = proj_out[phase - 4]
        wait(recv_sem.at[phase], slots.at[pl.ds(0, TEN - 1)])
        return jnp.sum(slots[...].astype(F32), axis=0)[:, 0:COLS]

    residual = rows + over_tensor(4, nt_dot(att, wo[...]), proj_in)

    square = jnp.sum(residual * residual, axis=1, keepdims=True)
    sq_out[0] = as_row(square)
    along_x_all(6, sq_out.at[0], sqfx_in)

    loads[12].wait()
    loads[14].wait()
    ffn_gated = (residual * gain2[...].astype(F32)[None, :]).astype(BF16)
    loads[9].wait()
    loads[10].wait()

    def partial(k, tiles):
        columns = pl.ds(pl.multiple_of(k * 256, 256), HEAD * tiles)
        gate = jnp.dot(ffn_gated, wg[:, columns], preferred_element_type=F32).astype(BF16)
        up = jnp.dot(ffn_gated, wu[:, columns], preferred_element_type=F32).astype(BF16)
        for a in range(2 * tiles):
            rows_of, columns_of = slice(a % 2 * 16, a % 2 * 16 + 16), slice(a // 2 * HEAD, a // 2 * HEAD + HEAD)
            gu_out[4 * k + a, 0:16, :] = gate[rows_of, columns_of]
            gu_out[4 * k + a, 16:32, :] = up[rows_of, columns_of]

    def along_x(n, k, i):
        a = ring_peer(x, i, 4)
        pltpu.make_async_remote_copy(
            src_ref=gu_out.at[4 * k + a],
            dst_ref=gx_in.at[n, i],
            send_sem=gx_send.at[n],
            recv_sem=gx_recv.at[n],
            device_id=(a * 8 + z, t),
            device_id_type=MESH,
        ).start()

    for n in range(3):
        partial(8 + n, 2 if n < 2 else 1)
        for i in range(3):
            if n < 2:
                along_x(n, 8 + n, i)
            else:

                @pl.when(ring_peer(x, i, 4) < 2)
                def _():
                    along_x(2, 10, i)

    @pl.loop(0, 8)
    def _(n):
        k = ring_peer(z, n)
        partial(k, 2)
        for i in range(3):
            along_x(3 + n, k, i)

    sq_out[1] = sum_of(6, sq_out.at[0], sqfx_in)
    along_z_all(10, sq_out.at[1], sqfz_in)

    def x_sum(n, k):
        wait(gx_recv.at[n], gx_in.at[n])
        total = gu_out[4 * k + x].astype(F32)
        for i in range(3):
            total = total + gx_in[n, i].astype(F32)
        return total.astype(BF16)

    for n in range(3):
        here = (x < 4) if n < 2 else (x < 2)

        @pl.when(here & (z == n))
        def _():
            gz_in2[z] = x_sum(n, 8 + n)

        @pl.when(here & (z != n))
        def _():
            gz_out[n] = x_sum(n, 8 + n)
            pltpu.make_async_remote_copy(
                src_ref=gz_out.at[n],
                dst_ref=gz_in2.at[z],
                send_sem=gz_send.at[n],
                recv_sem=recv_sem.at[8],
                device_id=(x * 8 + n, t),
                device_id_type=MESH,
            ).start()

    @pl.loop(0, 7)
    def _(n):
        k = ring_peer(z, n)
        gz_out[3 + n] = x_sum(3 + n, k)
        send(7, gz_out.at[3 + n], gz_in.at[n], (x * 8 + k, t))

    gz_in[7] = x_sum(10, z)
    leaves(7, gz_in.at[pl.ds(0, 7)])

    def sent_extra():
        for n in range(3):
            if n < 2:
                wait(gx_send.at[n], gx_in.at[n])
            else:

                @pl.when(x < 2)
                def _():
                    wait(gx_send.at[n], gx_in.at[n, pl.ds(0, 1)])

                @pl.when(x >= 2)
                def _():
                    wait(gx_send.at[n], gx_in.at[n, pl.ds(0, 2)])

            @pl.when(((x < 4) if n < 2 else (x < 2)) & (z != n))
            def _():
                wait(gz_send.at[n], gz_out.at[n])

        @pl.loop(3, 11)
        def _(n):
            wait(gx_send.at[n], gx_in.at[n])

    left.append(sent_extra)
    extra = (z < 2) | ((z == 2) & (x < 2))

    squares = sum_of(10, sq_out.at[1], sqfz_in)
    step_rows = iota((REQS, HEAD), 1) == iota((REQS, HEAD), 0) + REQS * (x % 2)
    squares = jnp.sum(jnp.where(step_rows, squares, 0.0), axis=1, keepdims=True)
    ffn_inv = lax.rsqrt(squares / WIDTH + EPS)
    levels = jnp.zeros((REQS, 1), jnp.int32)
    for r in range(REQS):
        levels = jnp.where(iota((REQS, 1), 0) == r, granularity[r], levels)
    active = levels > t

    def hidden_of(slots):
        both = jnp.sum(slots[...].astype(F32), axis=0)
        gate = both[0:16] * ffn_inv
        up = both[16:32] * ffn_inv
        act = 0.5 * gate * (1.0 + jnp.tanh(GELU * (gate + 0.044715 * (gate * gate * gate))))
        return jnp.where(active, act * up, 0.0).astype(BF16)

    owner = 4 * z + x

    def units(first, count):
        return hid_all.at[pl.ds(pl.multiple_of(first * 16, 16), count * 16)]

    def share(first, count):
        block = units(first, count)

        @pl.loop(0, CTX - 1)
        def _(i):
            send(9, block, block, (peer_of(x, z, i), t))

    @pl.when(extra)
    def _():
        wait(recv_sem.at[8], gz_in2.at[pl.ds(0, 7)])
        units(2 * owner + 1, 1)[...] = hidden_of(gz_in2)

    wait(recv_sem.at[7], gz_in.at[pl.ds(0, 7)])
    hidden_main = hidden_of(gz_in)

    @pl.when(extra)
    def _():
        units(2 * owner, 1)[...] = hidden_main
        share(2 * owner, 2)

    @pl.when(jnp.logical_not(extra))
    def _():
        units(owner + EXTRA, 1)[...] = hidden_main
        share(owner + EXTRA, 1)

    def hidden_left():
        @pl.when(extra)
        def _():
            wait(send_sem.at[9], kc.at[0, pl.ds(0, 32 * (CTX - 1))])

        @pl.when(jnp.logical_not(extra))
        def _():
            wait(send_sem.at[9], hid_all.at[pl.ds(0, 16 * (CTX - 1))])

    left.append(hidden_left)
    loads[11].wait()

    @pl.when(extra)
    def _():
        wait(recv_sem.at[9], hid_all.at[pl.ds(0, 16 * (CTX + EXTRA - 2))])

    @pl.when(jnp.logical_not(extra))
    def _():
        wait(recv_sem.at[9], hid_all.at[pl.ds(0, 16 * (CTX + EXTRA - 1))])

    def unit_at(unit):
        own = unit % CTX
        place = 2 * own + unit // CTX if own < EXTRA else own + EXTRA
        return hid_all[place * 16 : place * 16 + 16, :]

    hidden = jnp.concatenate(
        [
            jnp.concatenate([unit_at(2 * i), unit_at(2 * i + 1)], axis=0)
            for i in range(TILES)
        ],
        axis=1,
    )
    output = residual + over_tensor(5, nt_dot(hidden, wd[...]), down_in)
    out_ref[...] = output.astype(BF16)

    for sent in left:
        sent()


def per_device(
    first_input,
    second_input,
    attn_gain,
    query_weight,
    key_weight,
    value_weight,
    out_weight,
    ffn_gain,
    gate_weight,
    up_weight,
    down_weight,
    key_cache,
    value_cache,
    lengths,
    granularity,
):
    hbm = pl.BlockSpec(memory_space=pltpu.HBM)
    vmem = pl.BlockSpec(memory_space=pltpu.VMEM)
    V = pltpu.VMEM
    (both,) = pl.pallas_call(
        kernel,
        out_shape=(
            pltpu.VMEM((ROWS, COLS), BF16),
        ),
        in_specs=[hbm] * 15,
        out_specs=(vmem,),
        scratch_shapes=[
            pltpu.SMEM((REQS,), jnp.int32),
            pltpu.SMEM((REQS,), jnp.int32),
            V((REQS, COLS), BF16),
            V((REQS, COLS), BF16),
            V((COLS,), BF16),
            V((COLS,), BF16),
            V((COLS, 512), BF16),
            V((COLS, 256), BF16),
            V((COLS, 256), BF16),
            V((COLS, 512), BF16),
            V((COLS, 2688), BF16),
            V((COLS, 2688), BF16),
            V((COLS, 2688), BF16),
            V((REQS, 2 * POS, HEAD), BF16),
            V((REQS, 2 * POS, HEAD), BF16),
            V((4, REQS, 512), BF16),
            V((2, 3, REQS, 512), BF16),
            V((2, 7, REQS, 512), BF16),
            V((REQS * 8, HEAD), F32),
            V((CTX, 8, HEAD), F32),
            V((ROWS, HEAD), F32),
            V((2, 1, HEAD), F32),
            V((3, 1, HEAD), F32),
            V((7, 1, HEAD), F32),
            V((REQS * 8, HEAD), F32),
            V((REQS, 16, HEAD), BF16),
            V((CTX, 16, HEAD), BF16),
            V((REQS * 8, HEAD), F32),
            V((2, ROWS, 2 * HEAD), BF16),
            V((TEN, ROWS, 2 * HEAD), BF16),
            V((2, 1, HEAD), F32),
            V((3, 1, HEAD), F32),
            V((7, 1, HEAD), F32),
            V((2 * TILES, 32, HEAD), BF16),
            V((11, 3, 32, HEAD), BF16),
            V((10, 32, HEAD), BF16),
            V((8, 32, HEAD), BF16),
            V((8, 32, HEAD), BF16),
            V((TILES * ROWS, HEAD), BF16),
            V((TEN, ROWS, 2 * HEAD), BF16),
            pltpu.SemaphoreType.DMA((15,)),
            pltpu.SemaphoreType.DMA((17,)),
            pltpu.SemaphoreType.DMA((17,)),
            pltpu.SemaphoreType.DMA((11,)),
            pltpu.SemaphoreType.DMA((11,)),
            pltpu.SemaphoreType.DMA((3,)),
        ],
        compiler_params=pltpu.CompilerParams(
            collective_id=0, has_side_effects=True, vmem_limit_bytes=56 * 2**20
        ),
    )(
        lengths,
        granularity,
        first_input,
        second_input,
        attn_gain,
        ffn_gain,
        query_weight,
        key_weight,
        value_weight,
        out_weight.T,
        gate_weight,
        up_weight,
        down_weight.T,
        key_cache.reshape(REQS, 2 * POS, HEAD),
        value_cache.reshape(REQS, 2 * POS, HEAD),
    )
    return both[0:REQS], both[REQS:ROWS]


def solution(mesh):
    return jax.shard_map(
        per_device,
        mesh=mesh,
        in_specs=(
            P(None, "context"),
            P(None, "context"),
            P("context"),
            P("context", "tensor"),
            P("context", "tensor"),
            P("context", "tensor"),
            P("tensor", "context"),
            P("context"),
            P("context", "tensor"),
            P("context", "tensor"),
            P("tensor", "context"),
            P(None, "context", "tensor", None),
            P(None, "context", "tensor", None),
            P(),
            P(),
        ),
        out_specs=(P(None, "context"), P(None, "context")),
        check_vma=False,
    )
```

```python
import math

import jax
import jax.numpy as jnp
from jax import lax
from jax.experimental import pallas as pl
from jax.experimental.pallas import tpu as pltpu
from jax.sharding import PartitionSpec as P

EPS = 1e-06
MASKED = -1e30
WIDTH = 5376
COLS = 168
HEAD = 128
CTX = 32
TEN = 8
REQS = 16
ROWS = 32
POS = 512
TILES = 21
EXTRA = 10
SCALE = HEAD**-0.5
GELU = math.sqrt(2.0 / math.pi)
MESH = pl.DeviceIdType.MESH
F32 = jnp.float32
BF16 = jnp.bfloat16


def iota(shape, dim):
    return lax.broadcasted_iota(jnp.int32, shape, dim)


def ring_peer(me, i, size=8):
    return lax.rem(me + size // 2 + ((i + 1) // 2) * (1 - 2 * (i % 2)), size)


def peer_of(x, z, i):
    return ring_peer(x, i % 4, 4) * 8 + ring_peer(z, i // 4)


NEAR = [
    (0, 0),
    (0, 1),
    (0, 7),
    (1, 0),
    (3, 0),
    (2, 0),
    (0, 2),
    (0, 6),
    (1, 1),
    (1, 7),
    (3, 1),
    (3, 7),
    (0, 3),
    (0, 5),
    (1, 2),
    (1, 6),
]


def hops(offset):
    return min(offset[0], 4 - offset[0]) + min(offset[1], 8 - offset[1])


def opposite(offset):
    return ((offset[0] + 2) % 4, (offset[1] + 4) % 8)


def far_first(offsets):
    return sorted(offsets, key=hops, reverse=True)


def nt_dot(a, b):
    return lax.dot_general(a, b, (((1,), (1,)), ((), ())), preferred_element_type=F32)


def kernel(
    lengths_hbm,
    granularity_hbm,
    x1_hbm,
    x2_hbm,
    gain1_hbm,
    gain2_hbm,
    wq_hbm,
    wk_hbm,
    wv_hbm,
    wo_hbm,
    wg_hbm,
    wu_hbm,
    wd_hbm,
    kc_hbm,
    vc_hbm,
    out_ref,
    lengths,
    granularity,
    x1,
    x2,
    gain1,
    gain2,
    wq,
    wk,
    wv,
    wo,
    wg,
    wu,
    wd,
    kc,
    vc,
    qa_out,
    qb_out,
    qax_in,
    qaz_in,
    qbz_in,
    qbx_in,
    kv_part_rows,
    kv_out,
    kvx_in,
    kv_sum,
    kvz_in,
    inv_rows,
    new_sq,
    sqx_in,
    sqz_in,
    qkv_all,
    mix_out,
    mix_in,
    att_all,
    proj_out,
    proj_in,
    sq_out,
    sqfx_in,
    sqfz_in,
    gu_out,
    gx_in,
    gz_out,
    gz_in,
    gz_in2,
    hid_all,
    down_in,
    local_sem,
    send_sem,
    recv_sem,
    gx_send,
    gx_recv,
    gz_send,
):
    c = lax.axis_index("context")
    t = lax.axis_index("tensor")
    x, z = c // 8, c % 8

    def local(i, src, dst):
        return pltpu.make_async_copy(src, dst, local_sem.at[i])

    loads = [
        local(0, x1_hbm, x1),
        local(1, x2_hbm, x2),
        local(2, gain1_hbm, gain1),
        local(3, wq_hbm, wq),
        local(4, wk_hbm, wk),
        local(5, wv_hbm, wv),
        local(6, kc_hbm, kc),
        local(7, vc_hbm, vc),
        local(8, wo_hbm, wo),
        local(9, wg_hbm, wg),
        local(10, wu_hbm, wu),
        local(11, wd_hbm, wd),
        local(12, gain2_hbm, gain2),
        local(13, lengths_hbm, lengths),
        local(14, granularity_hbm, granularity),
    ]
    barrier = pltpu.get_barrier_semaphore()

    @pl.loop(0, 7)
    def _(i):
        pl.semaphore_signal(
            barrier, inc=1, device_id=(x * 8 + ring_peer(z, i), t), device_id_type=MESH
        )

    @pl.loop(0, 3)
    def _(i):
        pl.semaphore_signal(
            barrier, inc=1, device_id=(ring_peer(x, i, 4) * 8 + z, t), device_id_type=MESH
        )

    for load in loads[0:6]:
        load.start()

    @pl.loop(0, TEN - 1)
    def _(i):
        pl.semaphore_signal(
            barrier, inc=1, device_id=(c, ring_peer(t, i)), device_id_type=MESH
        )

    for load in loads[6:]:
        load.start()

    def send(phase, src, dst, peer):
        pltpu.make_async_remote_copy(
            src_ref=src,
            dst_ref=dst,
            send_sem=send_sem.at[phase],
            recv_sem=recv_sem.at[phase],
            device_id=peer,
            device_id_type=MESH,
        ).start()

    def wait(sem, ref):
        pltpu.make_async_copy(ref, ref, sem).wait()

    left = []

    def leaves(phase, ref):
        left.append(lambda: wait(send_sem.at[phase], ref))

    for i in range(6):
        loads[i].wait()
    rows = jnp.concatenate([x1[...], x2[...]], axis=0).astype(F32)
    gated = (rows * gain1[...].astype(F32)[None, :]).astype(BF16)
    q_part = jnp.dot(gated, wq[...], preferred_element_type=F32)
    k_part = jnp.dot(gated, wk[...], preferred_element_type=F32)
    v_part = jnp.dot(gated, wv[...], preferred_element_type=F32)
    qa_out[0] = q_part[0:REQS].astype(BF16)
    qb_out[0] = q_part[REQS:ROWS].astype(BF16)
    diagonal = iota((ROWS, HEAD), 0) == iota((ROWS, HEAD), 1)

    def as_row(column):
        return jnp.sum(jnp.where(diagonal, column, 0.0), axis=0, keepdims=True)

    def as_column(row):
        return jnp.sum(jnp.where(diagonal, row, 0.0), axis=1, keepdims=True)

    new_sq[0] = as_row(jnp.sum(rows * rows, axis=1, keepdims=True))

    pl.semaphore_wait(barrier, 7 + 3 + TEN - 1)

    def along_x_all(phase, src, slots):
        @pl.loop(0, 3)
        def _(i):
            send(phase, src, slots.at[i], (ring_peer(x, i, 4) * 8 + z, t))

        leaves(phase, slots)

    def along_z_all(phase, src, slots):
        @pl.loop(0, 7)
        def _(i):
            send(phase, src, slots.at[i], (x * 8 + ring_peer(z, i), t))

        leaves(phase, slots)

    def sum_of(phase, own, slots):
        wait(recv_sem.at[phase], slots)
        return own[...].astype(F32) + jnp.sum(slots[...].astype(F32), axis=0)

    def place(offset):
        return lax.rem(x + offset[0], 4), lax.rem(z + offset[1], 8)

    def request_at(at):
        return (at[0] % 2) * 8 + lax.rem(at[1] + 4 * (at[0] // 2), 8)

    along_z_all(1, qb_out.at[0], qbz_in)
    along_x_all(0, qa_out.at[0], qax_in)
    along_x_all(11, new_sq.at[0], sqx_in)

    kv_part = jnp.concatenate([k_part, v_part], axis=1)
    for s in range(2):
        for j in range(4):
            kv_part_rows[pl.ds(4 * s + j, REQS, stride=8), :] = kv_part[
                s * REQS : s * REQS + REQS, j * HEAD : (j + 1) * HEAD
            ]
    for parity in range(2):
        kv_out[parity] = kv_part_rows[64 * parity : 64 * parity + 64, :].astype(BF16)

    @pl.loop(0, 3)
    def _(i):
        a = ring_peer(x, i, 4)
        send(12, kv_out.at[a % 2], kvx_in.at[i], (a * 8 + z, t))

    leaves(12, kvx_in)
    qa_out[1] = sum_of(0, qa_out.at[0], qax_in).astype(BF16)
    along_z_all(13, qa_out.at[1], qaz_in)
    new_sq[1] = sum_of(11, new_sq.at[0], sqx_in)
    along_z_all(14, new_sq.at[1], sqz_in)
    qb_out[1] = sum_of(1, qb_out.at[0], qbz_in).astype(BF16)
    along_x_all(15, qb_out.at[1], qbx_in)
    kv_sum[...] = sum_of(12, kv_out.at[x % 2], kvx_in)

    def kv_rows(place_z):
        local_request = lax.rem(place_z + 4 * (x // 2), 8)
        return kv_sum.at[pl.ds(pl.multiple_of(local_request * 8, 8), 8)]

    @pl.loop(0, 7)
    def _(i):
        b = ring_peer(z, i)
        send(16, kv_rows(b), kvz_in.at[i], (x * 8 + b, t))

    leaves(16, kvz_in)
    squares = as_column(sum_of(14, new_sq.at[1], sqz_in))
    inv = lax.rsqrt(squares / WIDTH + EPS)
    inv_rows[...] = jnp.broadcast_to(inv, (ROWS, HEAD))
    part_b = sum_of(15, qb_out.at[1], qbx_in)
    part_a = sum_of(13, qa_out.at[1], qaz_in)
    totals = [part_a, part_b]
    for s in range(2):
        query = (totals[s] * inv[s * REQS : s * REQS + REQS]).astype(BF16).astype(F32)
        for j in range(4):
            start = (2 * j + s) * REQS
            qkv_all[start : start + REQS, :] = query[:, j * HEAD : (j + 1) * HEAD]

    loads[13].wait()
    loads[6].wait()
    loads[7].wait()
    lane = iota((8, 2 * POS), 1)
    own_head = (lane % 2) == (iota((8, 2 * POS), 0) // 4)
    position = c * POS + lane // 2

    lane = iota((8, HEAD), 1)
    for half in (NEAR[:8], NEAR[8:]):
        requests = [request_at(place(offset)) for offset in half]
        queries = [qkv_all[pl.ds(r, 8, stride=16), :].astype(BF16) for r in requests]
        scores = [nt_dot(q, kc[r]) * SCALE for q, r in zip(queries, requests)]
        live = [own_head & (position < lengths[r]) for r in requests]
        peaks = [
            jnp.max(jnp.where(l, s, MASKED), axis=1, keepdims=True) for s, l in zip(scores, live)
        ]
        weights = [
            jnp.where(l, jnp.exp(s - m), 0.0) for s, l, m in zip(scores, live, peaks)
        ]
        sums = [jnp.sum(w, axis=1, keepdims=True) for w in weights]
        mixtures = [
            jnp.dot(w.astype(BF16), vc[r], preferred_element_type=F32)
            for w, r in zip(weights, requests)
        ]
        for r, m, total, mixture in zip(requests, peaks, sums, mixtures):
            first = m.astype(BF16).astype(F32)
            second = (m - first).astype(BF16).astype(F32)
            total_first = total.astype(BF16).astype(F32)
            stats = jnp.where(lane == 3, total_first, total - total_first)
            stats = jnp.where(lane == 2, m - first - second, stats)
            stats = jnp.where(lane == 1, second, stats)
            stats = jnp.where(lane == 0, first, stats)
            stats = jnp.where(lane > 4, 0.0, stats)
            mix_out[r] = jnp.concatenate([mixture, stats], axis=0).astype(BF16)
        for offset in far_first(half + [opposite(offset) for offset in half]):
            if offset != (0, 0):
                a, b = place(offset)
                send(2, mix_out.at[request_at((a, b))], mix_in.at[c], (a * 8 + b, t))

    leaves(2, mix_in.at[pl.ds(0, CTX - 1)])

    request = request_at((x, z))
    mix_in[c] = mix_out[request]
    query = qkv_all[pl.ds(request, 8, stride=16), :]
    first_head = iota((8, 1), 0) < 4
    second_step = (iota((8, 1), 0) % 2) == 1
    inv_step = [inv_rows[pl.ds(s * REQS + request, 1), :] for s in range(2)]
    new = sum_of(16, kv_rows(z), kvz_in) * jnp.where(first_head, inv_step[0], inv_step[1])
    new = new.astype(BF16).astype(F32)

    def new_rows(j, s):
        return jnp.where(first_head, new[4 * s + j : 4 * s + j + 1], new[4 * s + j + 1 : 4 * s + j + 2])

    own = [jnp.sum(query * new_rows(0, s), axis=1, keepdims=True) * SCALE for s in range(2)]
    own[1] = jnp.where(second_step, own[1], MASKED)
    new_values = [new_rows(2, s) for s in range(2)]
    wait(recv_sem.at[2], mix_in.at[pl.ds(0, CTX - 1)])
    mixed = mix_in[:, 0:8, :].astype(F32)
    stats = mix_in[:, 8:16, :].astype(F32)
    lane = iota((CTX, 8, HEAD), 2)
    peaks = jnp.sum(jnp.where(lane < 3, stats, 0.0), axis=2, keepdims=True)
    sums = jnp.sum(jnp.where(lane < 3, 0.0, stats), axis=2, keepdims=True)
    highest = jnp.maximum(jnp.max(peaks, axis=0), jnp.maximum(own[0], own[1]))
    rescale = jnp.exp(peaks - highest[None])
    denominator = jnp.sum(rescale * sums, axis=0)
    numerator = jnp.sum(rescale * mixed, axis=0)
    own_weight = [
        jnp.exp(own[0] - highest),
        jnp.where(second_step, jnp.exp(own[1] - highest), 0.0),
    ]
    for s in range(2):
        denominator = denominator + own_weight[s]
        numerator = numerator + own_weight[s] * new_values[s]
    mine = att_all.at[pl.ds(pl.multiple_of(request * 8, 8), 8)]
    mine[...] = (numerator / denominator).astype(BF16).astype(F32)
    for offset in far_first(NEAR):
        if offset != (0, 0):
            a, b = place(offset)
            send(3, mine, mine, (a * 8 + b, t))

    leaves(3, att_all.at[pl.ds(0, 8 * (REQS - 1))])
    loads[8].wait()
    wait(recv_sem.at[3], att_all.at[pl.ds(0, 8 * (REQS - 1))])

    att = jnp.concatenate(
        [
            jnp.concatenate(
                [
                    att_all[pl.ds(2 * j + s, REQS, stride=8), :]
                    for s in range(2)
                ],
                axis=0,
            )
            for j in range(4)
        ],
        axis=1,
    ).astype(BF16)
    pad = jnp.zeros((ROWS, 2 * HEAD - COLS), F32)

    def over_tensor(phase, value, slots):
        proj_out[phase - 4] = jnp.concatenate([value, pad], axis=1).astype(BF16)

        @pl.loop(0, TEN - 1)
        def _(i):
            send(phase, proj_out.at[phase - 4], slots.at[t], (c, ring_peer(t, i)))

        if phase == 5:
            while left:
                left.pop(0)()
        leaves(phase, slots.at[pl.ds(0, TEN - 1)])

        slots[t] = proj_out[phase - 4]
        wait(recv_sem.at[phase], slots.at[pl.ds(0, TEN - 1)])
        return jnp.sum(slots[...].astype(F32), axis=0)[:, 0:COLS]

    residual = rows + over_tensor(4, nt_dot(att, wo[...]), proj_in)

    square = jnp.sum(residual * residual, axis=1, keepdims=True)
    sq_out[0] = as_row(square)
    along_x_all(6, sq_out.at[0], sqfx_in)

    loads[12].wait()
    loads[14].wait()
    ffn_gated = (residual * gain2[...].astype(F32)[None, :]).astype(BF16)
    loads[9].wait()
    loads[10].wait()

    def partial(k, tiles):
        columns = pl.ds(pl.multiple_of(k * 256, 256), HEAD * tiles)
        gate = jnp.dot(ffn_gated, wg[:, columns], preferred_element_type=F32).astype(BF16)
        up = jnp.dot(ffn_gated, wu[:, columns], preferred_element_type=F32).astype(BF16)
        for a in range(2 * tiles):
            rows_of, columns_of = slice(a % 2 * 16, a % 2 * 16 + 16), slice(a // 2 * HEAD, a // 2 * HEAD + HEAD)
            gu_out[4 * k + a, 0:16, :] = gate[rows_of, columns_of]
            gu_out[4 * k + a, 16:32, :] = up[rows_of, columns_of]

    def along_x(n, k, i):
        a = ring_peer(x, i, 4)
        pltpu.make_async_remote_copy(
            src_ref=gu_out.at[4 * k + a],
            dst_ref=gx_in.at[n, i],
            send_sem=gx_send.at[n],
            recv_sem=gx_recv.at[n],
            device_id=(a * 8 + z, t),
            device_id_type=MESH,
        ).start()

    @pl.loop(0, 8)
    def _(n):
        k = ring_peer(z, n)
        partial(k, 2)
        for i in range(3):
            along_x(k, k, i)

        @pl.when(k < 2)
        def _():
            partial(8 + k, 2)
            for i in range(3):
                along_x(8 + k, 8 + k, i)

        @pl.when(k == 2)
        def _():
            partial(10, 1)
            for i in range(3):

                @pl.when(ring_peer(x, i, 4) < 2)
                def _():
                    along_x(10, 10, i)

    sq_out[1] = sum_of(6, sq_out.at[0], sqfx_in)
    along_z_all(10, sq_out.at[1], sqfz_in)

    def x_sum(k):
        wait(gx_recv.at[k], gx_in.at[k])
        total = gu_out[4 * k + x].astype(F32)
        for i in range(3):
            total = total + gx_in[k, i].astype(F32)
        return total.astype(BF16)

    def to_owner(k, slot, send_from, recv_at):
        pltpu.make_async_remote_copy(
            src_ref=gz_out.at[k],
            dst_ref=slot,
            send_sem=send_from,
            recv_sem=recv_at,
            device_id=(x * 8 + k % 8, t),
            device_id_type=MESH,
        ).start()

    @pl.loop(0, 7)
    def _(n):
        k = ring_peer(z, n)
        gz_out[k] = x_sum(k)
        to_owner(k, gz_in.at[n], send_sem.at[7], recv_sem.at[7])

        @pl.when((k < 2) | ((k == 2) & (x < 2)))
        def _():
            gz_out[8 + k] = x_sum(8 + k)
            to_owner(8 + k, gz_in2.at[n], gz_send.at[k], recv_sem.at[8])

    gz_in[7] = x_sum(z)
    leaves(7, gz_in.at[pl.ds(0, 7)])
    extra = (z < 2) | ((z == 2) & (x < 2))

    @pl.when(extra)
    def _():
        gz_in2[7] = x_sum(8 + z)

    def sent_extra():
        @pl.loop(0, 10)
        def _(k):
            wait(gx_send.at[k], gx_in.at[k])

        @pl.when(x < 2)
        def _():
            wait(gx_send.at[10], gx_in.at[10, pl.ds(0, 1)])

        @pl.when(x >= 2)
        def _():
            wait(gx_send.at[10], gx_in.at[10, pl.ds(0, 2)])

        for k in range(3):

            @pl.when(((x < 4) if k < 2 else (x < 2)) & (z != k))
            def _():
                wait(gz_send.at[k], gz_out.at[8 + k])

    left.append(sent_extra)

    squares = sum_of(10, sq_out.at[1], sqfz_in)
    step_rows = iota((REQS, HEAD), 1) == iota((REQS, HEAD), 0) + REQS * (x % 2)
    squares = jnp.sum(jnp.where(step_rows, squares, 0.0), axis=1, keepdims=True)
    ffn_inv = lax.rsqrt(squares / WIDTH + EPS)
    levels = jnp.zeros((REQS, 1), jnp.int32)
    for r in range(REQS):
        levels = jnp.where(iota((REQS, 1), 0) == r, granularity[r], levels)
    active = levels > t

    def hidden_of(slots):
        both = jnp.sum(slots[...].astype(F32), axis=0)
        gate = both[0:16] * ffn_inv
        up = both[16:32] * ffn_inv
        act = 0.5 * gate * (1.0 + jnp.tanh(GELU * (gate + 0.044715 * (gate * gate * gate))))
        return jnp.where(active, act * up, 0.0).astype(BF16)

    owner = 4 * z + x

    def units(first, count):
        return hid_all.at[pl.ds(pl.multiple_of(first * 16, 16), count * 16)]

    def share(first, count):
        block = units(first, count)

        @pl.loop(0, CTX - 1)
        def _(i):
            send(9, block, block, (peer_of(x, z, i), t))

    @pl.when(extra)
    def _():
        wait(recv_sem.at[8], gz_in2.at[pl.ds(0, 7)])
        units(2 * owner + 1, 1)[...] = hidden_of(gz_in2)

    wait(recv_sem.at[7], gz_in.at[pl.ds(0, 7)])
    hidden_main = hidden_of(gz_in)

    @pl.when(extra)
    def _():
        units(2 * owner, 1)[...] = hidden_main
        share(2 * owner, 2)

    @pl.when(jnp.logical_not(extra))
    def _():
        units(owner + EXTRA, 1)[...] = hidden_main
        share(owner + EXTRA, 1)

    def hidden_left():
        @pl.when(extra)
        def _():
            wait(send_sem.at[9], kc.at[0, pl.ds(0, 32 * (CTX - 1))])

        @pl.when(jnp.logical_not(extra))
        def _():
            wait(send_sem.at[9], hid_all.at[pl.ds(0, 16 * (CTX - 1))])

    left.append(hidden_left)
    loads[11].wait()

    @pl.when(extra)
    def _():
        wait(recv_sem.at[9], hid_all.at[pl.ds(0, 16 * (CTX + EXTRA - 2))])

    @pl.when(jnp.logical_not(extra))
    def _():
        wait(recv_sem.at[9], hid_all.at[pl.ds(0, 16 * (CTX + EXTRA - 1))])

    def unit_at(unit):
        own = unit % CTX
        place = 2 * own + unit // CTX if own < EXTRA else own + EXTRA
        return hid_all[place * 16 : place * 16 + 16, :]

    hidden = jnp.concatenate(
        [
            jnp.concatenate([unit_at(2 * i), unit_at(2 * i + 1)], axis=0)
            for i in range(TILES)
        ],
        axis=1,
    )
    output = residual + over_tensor(5, nt_dot(hidden, wd[...]), down_in)
    out_ref[...] = output.astype(BF16)

    for sent in left:
        sent()


def per_device(
    first_input,
    second_input,
    attn_gain,
    query_weight,
    key_weight,
    value_weight,
    out_weight,
    ffn_gain,
    gate_weight,
    up_weight,
    down_weight,
    key_cache,
    value_cache,
    lengths,
    granularity,
):
    hbm = pl.BlockSpec(memory_space=pltpu.HBM)
    vmem = pl.BlockSpec(memory_space=pltpu.VMEM)
    V = pltpu.VMEM
    (both,) = pl.pallas_call(
        kernel,
        out_shape=(
            pltpu.VMEM((ROWS, COLS), BF16),
        ),
        in_specs=[hbm] * 15,
        out_specs=(vmem,),
        scratch_shapes=[
            pltpu.SMEM((REQS,), jnp.int32),
            pltpu.SMEM((REQS,), jnp.int32),
            V((REQS, COLS), BF16),
            V((REQS, COLS), BF16),
            V((COLS,), BF16),
            V((COLS,), BF16),
            V((COLS, 512), BF16),
            V((COLS, 256), BF16),
            V((COLS, 256), BF16),
            V((COLS, 512), BF16),
            V((COLS, 2688), BF16),
            V((COLS, 2688), BF16),
            V((COLS, 2688), BF16),
            V((REQS, 2 * POS, HEAD), BF16),
            V((REQS, 2 * POS, HEAD), BF16),
            V((2, REQS, 512), BF16),
            V((2, REQS, 512), BF16),
            V((3, REQS, 512), BF16),
            V((7, REQS, 512), BF16),
            V((7, REQS, 512), BF16),
            V((3, REQS, 512), BF16),
            V((REQS * 8, HEAD), F32),
            V((2, 64, HEAD), BF16),
            V((3, 64, HEAD), BF16),
            V((64, HEAD), F32),
            V((7, 8, HEAD), F32),
            V((ROWS, HEAD), F32),
            V((2, 1, HEAD), F32),
            V((3, 1, HEAD), F32),
            V((7, 1, HEAD), F32),
            V((REQS * 8, HEAD), F32),
            V((REQS, 16, HEAD), BF16),
            V((CTX, 16, HEAD), BF16),
            V((REQS * 8, HEAD), F32),
            V((2, ROWS, 2 * HEAD), BF16),
            V((TEN, ROWS, 2 * HEAD), BF16),
            V((2, 1, HEAD), F32),
            V((3, 1, HEAD), F32),
            V((7, 1, HEAD), F32),
            V((2 * TILES, 32, HEAD), BF16),
            V((11, 3, 32, HEAD), BF16),
            V((11, 32, HEAD), BF16),
            V((8, 32, HEAD), BF16),
            V((8, 32, HEAD), BF16),
            V((TILES * ROWS, HEAD), BF16),
            V((TEN, ROWS, 2 * HEAD), BF16),
            pltpu.SemaphoreType.DMA((15,)),
            pltpu.SemaphoreType.DMA((17,)),
            pltpu.SemaphoreType.DMA((17,)),
            pltpu.SemaphoreType.DMA((11,)),
            pltpu.SemaphoreType.DMA((11,)),
            pltpu.SemaphoreType.DMA((3,)),
        ],
        compiler_params=pltpu.CompilerParams(
            collective_id=0, has_side_effects=True, vmem_limit_bytes=56 * 2**20
        ),
    )(
        lengths,
        granularity,
        first_input,
        second_input,
        attn_gain,
        ffn_gain,
        query_weight,
        key_weight,
        value_weight,
        out_weight.T,
        gate_weight,
        up_weight,
        down_weight.T,
        key_cache.reshape(REQS, 2 * POS, HEAD),
        value_cache.reshape(REQS, 2 * POS, HEAD),
    )
    return both[0:REQS], both[REQS:ROWS]


def solution(mesh):
    return jax.shard_map(
        per_device,
        mesh=mesh,
        in_specs=(
            P(None, "context"),
            P(None, "context"),
            P("context"),
            P("context", "tensor"),
            P("context", "tensor"),
            P("context", "tensor"),
            P("tensor", "context"),
            P("context"),
            P("context", "tensor"),
            P("context", "tensor"),
            P("tensor", "context"),
            P(None, "context", "tensor", None),
            P(None, "context", "tensor", None),
            P(),
            P(),
        ),
        out_specs=(P(None, "context"), P(None, "context")),
        check_vma=False,
    )
```

```python
import math

import jax
import jax.numpy as jnp
from jax import lax
from jax.experimental import pallas as pl
from jax.experimental.pallas import tpu as pltpu
from jax.sharding import PartitionSpec as P

EPS = 1e-06
MASKED = -1e30
WIDTH = 5376
COLS = 168
HEAD = 128
CTX = 32
TEN = 8
REQS = 16
ROWS = 32
POS = 512
TILES = 21
EXTRA = 10
SCALE = HEAD**-0.5
GELU = math.sqrt(2.0 / math.pi)
MESH = pl.DeviceIdType.MESH
F32 = jnp.float32
BF16 = jnp.bfloat16


def iota(shape, dim):
    return lax.broadcasted_iota(jnp.int32, shape, dim)


def ring_peer(me, i, size=8):
    return lax.rem(me + size // 2 + ((i + 1) // 2) * (1 - 2 * (i % 2)), size)


def peer_of(x, z, i):
    return ring_peer(x, i % 4, 4) * 8 + ring_peer(z, i // 4)


NEAR = [
    (0, 0),
    (0, 1),
    (0, 7),
    (1, 0),
    (3, 0),
    (2, 0),
    (0, 2),
    (0, 6),
    (1, 1),
    (1, 7),
    (3, 1),
    (3, 7),
    (0, 3),
    (0, 5),
    (1, 2),
    (1, 6),
]


def hops(offset):
    return min(offset[0], 4 - offset[0]) + min(offset[1], 8 - offset[1])


def opposite(offset):
    return ((offset[0] + 2) % 4, (offset[1] + 4) % 8)


def far_first(offsets):
    return sorted(offsets, key=hops, reverse=True)


def nt_dot(a, b):
    return lax.dot_general(a, b, (((1,), (1,)), ((), ())), preferred_element_type=F32)


def kernel(
    lengths_hbm,
    granularity_hbm,
    x1_hbm,
    x2_hbm,
    gain1_hbm,
    gain2_hbm,
    wq_hbm,
    wk_hbm,
    wv_hbm,
    wo_hbm,
    wg_hbm,
    wu_hbm,
    wd_hbm,
    kc_hbm,
    vc_hbm,
    out_ref,
    lengths,
    granularity,
    x1,
    x2,
    gain1,
    gain2,
    wq,
    wk,
    wv,
    wo,
    wg,
    wu,
    wd,
    kc,
    vc,
    qa_out,
    qb_out,
    qax_in,
    qaz_in,
    qbz_in,
    qbx_in,
    kv_part_rows,
    kv_out,
    kvx_in,
    kv_sum,
    kvz_in,
    inv_rows,
    new_sq,
    sqx_in,
    sqz_in,
    qkv_all,
    mix_out,
    mix_in,
    att_all,
    proj_out,
    proj_in,
    sq_out,
    sqfx_in,
    sqfz_in,
    gu_out,
    gx_in,
    gz_out,
    gz_in,
    gz_in2,
    hid_all,
    down_in,
    local_sem,
    send_sem,
    recv_sem,
    gx_send,
    gx_recv,
    gz_send,
):
    c = lax.axis_index("context")
    t = lax.axis_index("tensor")
    x, z = c // 8, c % 8

    def local(i, src, dst):
        return pltpu.make_async_copy(src, dst, local_sem.at[i])

    loads = [
        local(0, x1_hbm, x1),
        local(1, x2_hbm, x2),
        local(2, gain1_hbm, gain1),
        local(3, wq_hbm, wq),
        local(4, wk_hbm, wk),
        local(5, wv_hbm, wv),
        local(6, kc_hbm, kc),
        local(7, vc_hbm, vc),
        local(8, wo_hbm, wo),
        local(9, wg_hbm, wg),
        local(10, wu_hbm, wu),
        local(11, wd_hbm, wd),
        local(12, gain2_hbm, gain2),
        local(13, lengths_hbm, lengths),
        local(14, granularity_hbm, granularity),
    ]
    barrier = pltpu.get_barrier_semaphore()

    @pl.loop(0, 7)
    def _(i):
        pl.semaphore_signal(
            barrier, inc=1, device_id=(x * 8 + ring_peer(z, i), t), device_id_type=MESH
        )

    @pl.loop(0, 3)
    def _(i):
        pl.semaphore_signal(
            barrier, inc=1, device_id=(ring_peer(x, i, 4) * 8 + z, t), device_id_type=MESH
        )

    for load in loads[0:6]:
        load.start()

    @pl.loop(0, TEN - 1)
    def _(i):
        pl.semaphore_signal(
            barrier, inc=1, device_id=(c, ring_peer(t, i)), device_id_type=MESH
        )

    for load in loads[6:]:
        load.start()

    def send(phase, src, dst, peer):
        pltpu.make_async_remote_copy(
            src_ref=src,
            dst_ref=dst,
            send_sem=send_sem.at[phase],
            recv_sem=recv_sem.at[phase],
            device_id=peer,
            device_id_type=MESH,
        ).start()

    def wait(sem, ref):
        pltpu.make_async_copy(ref, ref, sem).wait()

    left = []

    def leaves(phase, ref):
        left.append(lambda: wait(send_sem.at[phase], ref))

    for i in range(6):
        loads[i].wait()
    rows = jnp.concatenate([x1[...], x2[...]], axis=0).astype(F32)
    gated = (rows * gain1[...].astype(F32)[None, :]).astype(BF16)
    q_part = jnp.dot(gated, wq[...], preferred_element_type=F32)
    k_part = jnp.dot(gated, wk[...], preferred_element_type=F32)
    v_part = jnp.dot(gated, wv[...], preferred_element_type=F32)
    qa_out[0] = q_part[0:REQS].astype(BF16)
    qb_out[0] = q_part[REQS:ROWS].astype(BF16)
    diagonal = iota((ROWS, HEAD), 0) == iota((ROWS, HEAD), 1)

    def as_row(column):
        return jnp.sum(jnp.where(diagonal, column, 0.0), axis=0, keepdims=True)

    def as_column(row):
        return jnp.sum(jnp.where(diagonal, row, 0.0), axis=1, keepdims=True)

    new_sq[0] = as_row(jnp.sum(rows * rows, axis=1, keepdims=True))

    pl.semaphore_wait(barrier, 7 + 3 + TEN - 1)

    def along_x_all(phase, src, slots):
        @pl.loop(0, 3)
        def _(i):
            send(phase, src, slots.at[i], (ring_peer(x, i, 4) * 8 + z, t))

        leaves(phase, slots)

    def along_z_all(phase, src, slots):
        @pl.loop(0, 7)
        def _(i):
            send(phase, src, slots.at[i], (x * 8 + ring_peer(z, i), t))

        leaves(phase, slots)

    def sum_of(phase, own, slots):
        wait(recv_sem.at[phase], slots)
        return own[...].astype(F32) + jnp.sum(slots[...].astype(F32), axis=0)

    def place(offset):
        return lax.rem(x + offset[0], 4), lax.rem(z + offset[1], 8)

    def request_at(at):
        return (at[0] % 2) * 8 + lax.rem(at[1] + 4 * (at[0] // 2), 8)

    along_x_all(11, new_sq.at[0], sqx_in)
    along_x_all(0, qa_out.at[0], qax_in)
    along_z_all(1, qb_out.at[0], qbz_in)

    kv_part = jnp.concatenate([k_part, v_part], axis=1)
    for s in range(2):
        for j in range(4):
            kv_part_rows[pl.ds(4 * s + j, REQS, stride=8), :] = kv_part[
                s * REQS : s * REQS + REQS, j * HEAD : (j + 1) * HEAD
            ]
    for parity in range(2):
        kv_out[parity] = kv_part_rows[64 * parity : 64 * parity + 64, :].astype(BF16)

    @pl.loop(0, 3)
    def _(i):
        a = ring_peer(x, i, 4)
        send(12, kv_out.at[a % 2], kvx_in.at[i], (a * 8 + z, t))

    leaves(12, kvx_in)
    new_sq[1] = sum_of(11, new_sq.at[0], sqx_in)
    along_z_all(14, new_sq.at[1], sqz_in)
    qa_out[1] = sum_of(0, qa_out.at[0], qax_in).astype(BF16)
    along_z_all(13, qa_out.at[1], qaz_in)
    qb_out[1] = sum_of(1, qb_out.at[0], qbz_in).astype(BF16)
    along_x_all(15, qb_out.at[1], qbx_in)
    kv_sum[...] = sum_of(12, kv_out.at[x % 2], kvx_in)

    def kv_rows(place_z):
        local_request = lax.rem(place_z + 4 * (x // 2), 8)
        return kv_sum.at[pl.ds(pl.multiple_of(local_request * 8, 8), 8)]

    @pl.loop(0, 7)
    def _(i):
        b = ring_peer(z, i)
        send(16, kv_rows(b), kvz_in.at[i], (x * 8 + b, t))

    leaves(16, kvz_in)
    squares = as_column(sum_of(14, new_sq.at[1], sqz_in))
    inv = lax.rsqrt(squares / WIDTH + EPS)
    inv_rows[...] = jnp.broadcast_to(inv, (ROWS, HEAD))
    part_b = sum_of(15, qb_out.at[1], qbx_in)
    part_a = sum_of(13, qa_out.at[1], qaz_in)
    totals = [part_a, part_b]
    for s in range(2):
        query = (totals[s] * inv[s * REQS : s * REQS + REQS]).astype(BF16).astype(F32)
        for j in range(4):
            start = (2 * j + s) * REQS
            qkv_all[start : start + REQS, :] = query[:, j * HEAD : (j + 1) * HEAD]

    loads[13].wait()
    loads[6].wait()
    loads[7].wait()
    lane = iota((8, 2 * POS), 1)
    own_head = (lane % 2) == (iota((8, 2 * POS), 0) // 4)
    position = c * POS + lane // 2

    lane = iota((8, HEAD), 1)
    for half in (NEAR[:8], NEAR[8:]):
        requests = [request_at(place(offset)) for offset in half]
        queries = [qkv_all[pl.ds(r, 8, stride=16), :].astype(BF16) for r in requests]
        scores = [nt_dot(q, kc[r]) * SCALE for q, r in zip(queries, requests)]
        live = [own_head & (position < lengths[r]) for r in requests]
        peaks = [
            jnp.max(jnp.where(l, s, MASKED), axis=1, keepdims=True) for s, l in zip(scores, live)
        ]
        weights = [
            jnp.where(l, jnp.exp(s - m), 0.0) for s, l, m in zip(scores, live, peaks)
        ]
        sums = [jnp.sum(w, axis=1, keepdims=True) for w in weights]
        mixtures = [
            jnp.dot(w.astype(BF16), vc[r], preferred_element_type=F32)
            for w, r in zip(weights, requests)
        ]
        for r, m, total, mixture in zip(requests, peaks, sums, mixtures):
            first = m.astype(BF16).astype(F32)
            second = (m - first).astype(BF16).astype(F32)
            total_first = total.astype(BF16).astype(F32)
            stats = jnp.where(lane == 3, total_first, total - total_first)
            stats = jnp.where(lane == 2, m - first - second, stats)
            stats = jnp.where(lane == 1, second, stats)
            stats = jnp.where(lane == 0, first, stats)
            stats = jnp.where(lane > 4, 0.0, stats)
            mix_out[r] = jnp.concatenate([mixture, stats], axis=0).astype(BF16)
        for offset in far_first(half + [opposite(offset) for offset in half]):
            if offset != (0, 0):
                a, b = place(offset)
                send(2, mix_out.at[request_at((a, b))], mix_in.at[c], (a * 8 + b, t))

    leaves(2, mix_in.at[pl.ds(0, CTX - 1)])

    request = request_at((x, z))
    mix_in[c] = mix_out[request]
    query = qkv_all[pl.ds(request, 8, stride=16), :]
    first_head = iota((8, 1), 0) < 4
    second_step = (iota((8, 1), 0) % 2) == 1
    inv_step = [inv_rows[pl.ds(s * REQS + request, 1), :] for s in range(2)]
    new = sum_of(16, kv_rows(z), kvz_in) * jnp.where(first_head, inv_step[0], inv_step[1])
    new = new.astype(BF16).astype(F32)

    def new_rows(j, s):
        return jnp.where(first_head, new[4 * s + j : 4 * s + j + 1], new[4 * s + j + 1 : 4 * s + j + 2])

    own = [jnp.sum(query * new_rows(0, s), axis=1, keepdims=True) * SCALE for s in range(2)]
    own[1] = jnp.where(second_step, own[1], MASKED)
    new_values = [new_rows(2, s) for s in range(2)]
    wait(recv_sem.at[2], mix_in.at[pl.ds(0, CTX - 1)])
    mixed = mix_in[:, 0:8, :].astype(F32)
    stats = mix_in[:, 8:16, :].astype(F32)
    lane = iota((CTX, 8, HEAD), 2)
    peaks = jnp.sum(jnp.where(lane < 3, stats, 0.0), axis=2, keepdims=True)
    sums = jnp.sum(jnp.where(lane < 3, 0.0, stats), axis=2, keepdims=True)
    highest = jnp.maximum(jnp.max(peaks, axis=0), jnp.maximum(own[0], own[1]))
    rescale = jnp.exp(peaks - highest[None])
    denominator = jnp.sum(rescale * sums, axis=0)
    numerator = jnp.sum(rescale * mixed, axis=0)
    own_weight = [
        jnp.exp(own[0] - highest),
        jnp.where(second_step, jnp.exp(own[1] - highest), 0.0),
    ]
    for s in range(2):
        denominator = denominator + own_weight[s]
        numerator = numerator + own_weight[s] * new_values[s]
    mine = att_all.at[pl.ds(pl.multiple_of(request * 8, 8), 8)]
    mine[...] = (numerator / denominator).astype(BF16).astype(F32)
    for offset in far_first(NEAR):
        if offset != (0, 0):
            a, b = place(offset)
            send(3, mine, mine, (a * 8 + b, t))

    leaves(3, att_all.at[pl.ds(0, 8 * (REQS - 1))])
    loads[8].wait()
    wait(recv_sem.at[3], att_all.at[pl.ds(0, 8 * (REQS - 1))])

    att = jnp.concatenate(
        [
            jnp.concatenate(
                [
                    att_all[pl.ds(2 * j + s, REQS, stride=8), :]
                    for s in range(2)
                ],
                axis=0,
            )
            for j in range(4)
        ],
        axis=1,
    ).astype(BF16)
    pad = jnp.zeros((ROWS, 2 * HEAD - COLS), F32)

    def over_tensor(phase, value, slots):
        proj_out[phase - 4] = jnp.concatenate([value, pad], axis=1).astype(BF16)

        @pl.loop(0, TEN - 1)
        def _(i):
            send(phase, proj_out.at[phase - 4], slots.at[t], (c, ring_peer(t, i)))

        if phase == 5:
            while left:
                left.pop(0)()
        leaves(phase, slots.at[pl.ds(0, TEN - 1)])

        slots[t] = proj_out[phase - 4]
        wait(recv_sem.at[phase], slots.at[pl.ds(0, TEN - 1)])
        return jnp.sum(slots[...].astype(F32), axis=0)[:, 0:COLS]

    residual = rows + over_tensor(4, nt_dot(att, wo[...]), proj_in)

    square = jnp.sum(residual * residual, axis=1, keepdims=True)
    sq_out[0] = as_row(square)
    along_x_all(6, sq_out.at[0], sqfx_in)

    loads[12].wait()
    loads[14].wait()
    ffn_gated = (residual * gain2[...].astype(F32)[None, :]).astype(BF16)
    loads[9].wait()
    loads[10].wait()

    def partial(k, tiles):
        columns = pl.ds(pl.multiple_of(k * 256, 256), HEAD * tiles)
        gate = jnp.dot(ffn_gated, wg[:, columns], preferred_element_type=F32).astype(BF16)
        up = jnp.dot(ffn_gated, wu[:, columns], preferred_element_type=F32).astype(BF16)
        for a in range(2 * tiles):
            rows_of, columns_of = slice(a % 2 * 16, a % 2 * 16 + 16), slice(a // 2 * HEAD, a // 2 * HEAD + HEAD)
            gu_out[4 * k + a, 0:16, :] = gate[rows_of, columns_of]
            gu_out[4 * k + a, 16:32, :] = up[rows_of, columns_of]

    def along_x(n, k, i):
        a = ring_peer(x, i, 4)
        pltpu.make_async_remote_copy(
            src_ref=gu_out.at[4 * k + a],
            dst_ref=gx_in.at[n, i],
            send_sem=gx_send.at[n],
            recv_sem=gx_recv.at[n],
            device_id=(a * 8 + z, t),
            device_id_type=MESH,
        ).start()

    @pl.loop(0, 8)
    def _(n):
        k = ring_peer(z, n)
        partial(k, 2)
        for i in range(3):
            along_x(k, k, i)

        @pl.when(k < 2)
        def _():
            partial(8 + k, 2)
            for i in range(3):
                along_x(8 + k, 8 + k, i)

        @pl.when(k == 2)
        def _():
            partial(10, 1)
            for i in range(3):

                @pl.when(ring_peer(x, i, 4) < 2)
                def _():
                    along_x(10, 10, i)

    sq_out[1] = sum_of(6, sq_out.at[0], sqfx_in)
    along_z_all(10, sq_out.at[1], sqfz_in)

    def x_sum(k):
        wait(gx_recv.at[k], gx_in.at[k])
        total = gu_out[4 * k + x].astype(F32)
        for i in range(3):
            total = total + gx_in[k, i].astype(F32)
        return total.astype(BF16)

    def to_owner(k, slot, send_from, recv_at):
        pltpu.make_async_remote_copy(
            src_ref=gz_out.at[k],
            dst_ref=slot,
            send_sem=send_from,
            recv_sem=recv_at,
            device_id=(x * 8 + k % 8, t),
            device_id_type=MESH,
        ).start()

    @pl.loop(0, 7)
    def _(n):
        k = ring_peer(z, n)
        gz_out[k] = x_sum(k)
        to_owner(k, gz_in.at[n], send_sem.at[7], recv_sem.at[7])

        @pl.when((k < 2) | ((k == 2) & (x < 2)))
        def _():
            gz_out[8 + k] = x_sum(8 + k)
            to_owner(8 + k, gz_in2.at[n], gz_send.at[k], recv_sem.at[8])

    gz_in[7] = x_sum(z)
    leaves(7, gz_in.at[pl.ds(0, 7)])
    extra = (z < 2) | ((z == 2) & (x < 2))

    @pl.when(extra)
    def _():
        gz_in2[7] = x_sum(8 + z)

    def sent_extra():
        @pl.loop(0, 10)
        def _(k):
            wait(gx_send.at[k], gx_in.at[k])

        @pl.when(x < 2)
        def _():
            wait(gx_send.at[10], gx_in.at[10, pl.ds(0, 1)])

        @pl.when(x >= 2)
        def _():
            wait(gx_send.at[10], gx_in.at[10, pl.ds(0, 2)])

        for k in range(3):

            @pl.when(((x < 4) if k < 2 else (x < 2)) & (z != k))
            def _():
                wait(gz_send.at[k], gz_out.at[8 + k])

    left.append(sent_extra)

    squares = sum_of(10, sq_out.at[1], sqfz_in)
    step_rows = iota((REQS, HEAD), 1) == iota((REQS, HEAD), 0) + REQS * (x % 2)
    squares = jnp.sum(jnp.where(step_rows, squares, 0.0), axis=1, keepdims=True)
    ffn_inv = lax.rsqrt(squares / WIDTH + EPS)
    levels = jnp.zeros((REQS, 1), jnp.int32)
    for r in range(REQS):
        levels = jnp.where(iota((REQS, 1), 0) == r, granularity[r], levels)
    active = levels > t

    def hidden_of(slots):
        both = jnp.sum(slots[...].astype(F32), axis=0)
        gate = both[0:16] * ffn_inv
        up = both[16:32] * ffn_inv
        act = 0.5 * gate * (1.0 + jnp.tanh(GELU * (gate + 0.044715 * (gate * gate * gate))))
        return jnp.where(active, act * up, 0.0).astype(BF16)

    owner = 4 * z + x

    def units(first, count):
        return hid_all.at[pl.ds(pl.multiple_of(first * 16, 16), count * 16)]

    def share(first, count):
        block = units(first, count)

        @pl.loop(0, CTX - 1)
        def _(i):
            send(9, block, block, (peer_of(x, z, i), t))

    @pl.when(extra)
    def _():
        wait(recv_sem.at[8], gz_in2.at[pl.ds(0, 7)])
        units(2 * owner + 1, 1)[...] = hidden_of(gz_in2)

    wait(recv_sem.at[7], gz_in.at[pl.ds(0, 7)])
    hidden_main = hidden_of(gz_in)

    @pl.when(extra)
    def _():
        units(2 * owner, 1)[...] = hidden_main
        share(2 * owner, 2)

    @pl.when(jnp.logical_not(extra))
    def _():
        units(owner + EXTRA, 1)[...] = hidden_main
        share(owner + EXTRA, 1)

    def hidden_left():
        @pl.when(extra)
        def _():
            wait(send_sem.at[9], kc.at[0, pl.ds(0, 32 * (CTX - 1))])

        @pl.when(jnp.logical_not(extra))
        def _():
            wait(send_sem.at[9], hid_all.at[pl.ds(0, 16 * (CTX - 1))])

    left.append(hidden_left)
    loads[11].wait()

    @pl.when(extra)
    def _():
        wait(recv_sem.at[9], hid_all.at[pl.ds(0, 16 * (CTX + EXTRA - 2))])

    @pl.when(jnp.logical_not(extra))
    def _():
        wait(recv_sem.at[9], hid_all.at[pl.ds(0, 16 * (CTX + EXTRA - 1))])

    def unit_at(unit):
        own = unit % CTX
        place = 2 * own + unit // CTX if own < EXTRA else own + EXTRA
        return hid_all[place * 16 : place * 16 + 16, :]

    hidden = jnp.concatenate(
        [
            jnp.concatenate([unit_at(2 * i), unit_at(2 * i + 1)], axis=0)
            for i in range(TILES)
        ],
        axis=1,
    )
    output = residual + over_tensor(5, nt_dot(hidden, wd[...]), down_in)
    out_ref[...] = output.astype(BF16)

    for sent in left:
        sent()


def per_device(
    first_input,
    second_input,
    attn_gain,
    query_weight,
    key_weight,
    value_weight,
    out_weight,
    ffn_gain,
    gate_weight,
    up_weight,
    down_weight,
    key_cache,
    value_cache,
    lengths,
    granularity,
):
    hbm = pl.BlockSpec(memory_space=pltpu.HBM)
    vmem = pl.BlockSpec(memory_space=pltpu.VMEM)
    V = pltpu.VMEM
    (both,) = pl.pallas_call(
        kernel,
        out_shape=(
            pltpu.VMEM((ROWS, COLS), BF16),
        ),
        in_specs=[hbm] * 15,
        out_specs=(vmem,),
        scratch_shapes=[
            pltpu.SMEM((REQS,), jnp.int32),
            pltpu.SMEM((REQS,), jnp.int32),
            V((REQS, COLS), BF16),
            V((REQS, COLS), BF16),
            V((COLS,), BF16),
            V((COLS,), BF16),
            V((COLS, 512), BF16),
            V((COLS, 256), BF16),
            V((COLS, 256), BF16),
            V((COLS, 512), BF16),
            V((COLS, 2688), BF16),
            V((COLS, 2688), BF16),
            V((COLS, 2688), BF16),
            V((REQS, 2 * POS, HEAD), BF16),
            V((REQS, 2 * POS, HEAD), BF16),
            V((2, REQS, 512), BF16),
            V((2, REQS, 512), BF16),
            V((3, REQS, 512), BF16),
            V((7, REQS, 512), BF16),
            V((7, REQS, 512), BF16),
            V((3, REQS, 512), BF16),
            V((REQS * 8, HEAD), F32),
            V((2, 64, HEAD), BF16),
            V((3, 64, HEAD), BF16),
            V((64, HEAD), F32),
            V((7, 8, HEAD), F32),
            V((ROWS, HEAD), F32),
            V((2, 1, HEAD), F32),
            V((3, 1, HEAD), F32),
            V((7, 1, HEAD), F32),
            V((REQS * 8, HEAD), F32),
            V((REQS, 16, HEAD), BF16),
            V((CTX, 16, HEAD), BF16),
            V((REQS * 8, HEAD), F32),
            V((2, ROWS, 2 * HEAD), BF16),
            V((TEN, ROWS, 2 * HEAD), BF16),
            V((2, 1, HEAD), F32),
            V((3, 1, HEAD), F32),
            V((7, 1, HEAD), F32),
            V((2 * TILES, 32, HEAD), BF16),
            V((11, 3, 32, HEAD), BF16),
            V((11, 32, HEAD), BF16),
            V((8, 32, HEAD), BF16),
            V((8, 32, HEAD), BF16),
            V((TILES * ROWS, HEAD), BF16),
            V((TEN, ROWS, 2 * HEAD), BF16),
            pltpu.SemaphoreType.DMA((15,)),
            pltpu.SemaphoreType.DMA((17,)),
            pltpu.SemaphoreType.DMA((17,)),
            pltpu.SemaphoreType.DMA((11,)),
            pltpu.SemaphoreType.DMA((11,)),
            pltpu.SemaphoreType.DMA((3,)),
        ],
        compiler_params=pltpu.CompilerParams(
            collective_id=0, has_side_effects=True, vmem_limit_bytes=56 * 2**20
        ),
    )(
        lengths,
        granularity,
        first_input,
        second_input,
        attn_gain,
        ffn_gain,
        query_weight,
        key_weight,
        value_weight,
        out_weight.T,
        gate_weight,
        up_weight,
        down_weight.T,
        key_cache.reshape(REQS, 2 * POS, HEAD),
        value_cache.reshape(REQS, 2 * POS, HEAD),
    )
    return both[0:REQS], both[REQS:ROWS]


def solution(mesh):
    return jax.shard_map(
        per_device,
        mesh=mesh,
        in_specs=(
            P(None, "context"),
            P(None, "context"),
            P("context"),
            P("context", "tensor"),
            P("context", "tensor"),
            P("context", "tensor"),
            P("tensor", "context"),
            P("context"),
            P("context", "tensor"),
            P("context", "tensor"),
            P("tensor", "context"),
            P(None, "context", "tensor", None),
            P(None, "context", "tensor", None),
            P(),
            P(),
        ),
        out_specs=(P(None, "context"), P(None, "context")),
        check_vma=False,
    )
```

```python
import math

import jax
import jax.numpy as jnp
from jax import lax
from jax.experimental import pallas as pl
from jax.experimental.pallas import tpu as pltpu
from jax.sharding import PartitionSpec as P

EPS = 1e-06
MASKED = -1e30
WIDTH = 5376
COLS = 168
HEAD = 128
CTX = 32
TEN = 8
REQS = 16
ROWS = 32
POS = 512
TILES = 21
EXTRA = 10
SCALE = HEAD**-0.5
GELU = math.sqrt(2.0 / math.pi)
MESH = pl.DeviceIdType.MESH
F32 = jnp.float32
BF16 = jnp.bfloat16


def iota(shape, dim):
    return lax.broadcasted_iota(jnp.int32, shape, dim)


def ring_peer(me, i, size=8):
    return lax.rem(me + size // 2 + ((i + 1) // 2) * (1 - 2 * (i % 2)), size)


def peer_of(x, z, i):
    return ring_peer(x, i % 4, 4) * 8 + ring_peer(z, i // 4)


NEAR = [
    (0, 0),
    (0, 1),
    (0, 7),
    (1, 0),
    (3, 0),
    (2, 0),
    (0, 2),
    (0, 6),
    (1, 1),
    (1, 7),
    (3, 1),
    (3, 7),
    (0, 3),
    (0, 5),
    (1, 2),
    (1, 6),
]


def hops(offset):
    return min(offset[0], 4 - offset[0]) + min(offset[1], 8 - offset[1])


def opposite(offset):
    return ((offset[0] + 2) % 4, (offset[1] + 4) % 8)


def far_first(offsets):
    return sorted(offsets, key=hops, reverse=True)


def nt_dot(a, b):
    return lax.dot_general(a, b, (((1,), (1,)), ((), ())), preferred_element_type=F32)


def kernel(
    lengths_hbm,
    granularity_hbm,
    x1_hbm,
    x2_hbm,
    gain1_hbm,
    gain2_hbm,
    wq_hbm,
    wk_hbm,
    wv_hbm,
    wo_hbm,
    wg_hbm,
    wu_hbm,
    wd_hbm,
    kc_hbm,
    vc_hbm,
    out_ref,
    lengths,
    granularity,
    x1,
    x2,
    gain1,
    gain2,
    wq,
    wk,
    wv,
    wo,
    wg,
    wu,
    wd,
    kc,
    vc,
    kt,
    qa_out,
    qb_out,
    qax_in,
    qaz_in,
    qbz_in,
    qbx_in,
    kv_part_rows,
    kv_out,
    kvx_in,
    kv_sum,
    kvz_in,
    inv_rows,
    new_sq,
    sqx_in,
    sqz_in,
    qkv_all,
    mix_out,
    mix_in,
    att_all,
    proj_out,
    proj_in,
    sq_out,
    sqfx_in,
    sqfz_in,
    gu_out,
    gx_in,
    gz_out,
    gz_in,
    gz_in2,
    hid_all,
    down_in,
    local_sem,
    send_sem,
    recv_sem,
    gx_send,
    gx_recv,
    gz_send,
):
    c = lax.axis_index("context")
    t = lax.axis_index("tensor")
    x, z = c // 8, c % 8

    def local(i, src, dst):
        return pltpu.make_async_copy(src, dst, local_sem.at[i])

    loads = [
        local(0, x1_hbm, x1),
        local(1, x2_hbm, x2),
        local(2, gain1_hbm, gain1),
        local(3, wq_hbm, wq),
        local(4, wk_hbm, wk),
        local(5, wv_hbm, wv),
        local(6, kc_hbm, kc),
        local(7, vc_hbm, vc),
        local(8, wo_hbm, wo),
        local(9, wg_hbm, wg),
        local(10, wu_hbm, wu),
        local(11, wd_hbm, wd),
        local(12, gain2_hbm, gain2),
        local(13, lengths_hbm, lengths),
        local(14, granularity_hbm, granularity),
    ]
    barrier = pltpu.get_barrier_semaphore()

    @pl.loop(0, 7)
    def _(i):
        pl.semaphore_signal(
            barrier, inc=1, device_id=(x * 8 + ring_peer(z, i), t), device_id_type=MESH
        )

    @pl.loop(0, 3)
    def _(i):
        pl.semaphore_signal(
            barrier, inc=1, device_id=(ring_peer(x, i, 4) * 8 + z, t), device_id_type=MESH
        )

    for load in loads[0:6]:
        load.start()

    @pl.loop(0, TEN - 1)
    def _(i):
        pl.semaphore_signal(
            barrier, inc=1, device_id=(c, ring_peer(t, i)), device_id_type=MESH
        )

    for load in loads[6:]:
        load.start()

    def send(phase, src, dst, peer):
        pltpu.make_async_remote_copy(
            src_ref=src,
            dst_ref=dst,
            send_sem=send_sem.at[phase],
            recv_sem=recv_sem.at[phase],
            device_id=peer,
            device_id_type=MESH,
        ).start()

    def wait(sem, ref):
        pltpu.make_async_copy(ref, ref, sem).wait()

    left = []

    def leaves(phase, ref):
        left.append(lambda: wait(send_sem.at[phase], ref))

    for i in range(6):
        loads[i].wait()
    rows = jnp.concatenate([x1[...], x2[...]], axis=0).astype(F32)
    gated = (rows * gain1[...].astype(F32)[None, :]).astype(BF16)
    q_part = jnp.dot(gated, wq[...], preferred_element_type=F32)
    k_part = jnp.dot(gated, wk[...], preferred_element_type=F32)
    v_part = jnp.dot(gated, wv[...], preferred_element_type=F32)
    qa_out[0] = q_part[0:REQS].astype(BF16)
    qb_out[0] = q_part[REQS:ROWS].astype(BF16)
    diagonal = iota((ROWS, HEAD), 0) == iota((ROWS, HEAD), 1)

    def as_row(column):
        return jnp.sum(jnp.where(diagonal, column, 0.0), axis=0, keepdims=True)

    def as_column(row):
        return jnp.sum(jnp.where(diagonal, row, 0.0), axis=1, keepdims=True)

    new_sq[0] = as_row(jnp.sum(rows * rows, axis=1, keepdims=True))

    pl.semaphore_wait(barrier, 7 + 3 + TEN - 1)

    def along_x_all(phase, src, slots):
        @pl.loop(0, 3)
        def _(i):
            send(phase, src, slots.at[i], (ring_peer(x, i, 4) * 8 + z, t))

        leaves(phase, slots)

    def along_z_all(phase, src, slots):
        @pl.loop(0, 7)
        def _(i):
            send(phase, src, slots.at[i], (x * 8 + ring_peer(z, i), t))

        leaves(phase, slots)

    def sum_of(phase, own, slots):
        wait(recv_sem.at[phase], slots)
        return own[...].astype(F32) + jnp.sum(slots[...].astype(F32), axis=0)

    def place(offset):
        return lax.rem(x + offset[0], 4), lax.rem(z + offset[1], 8)

    def request_at(at):
        return (at[0] % 2) * 8 + lax.rem(at[1] + 4 * (at[0] // 2), 8)

    along_x_all(11, new_sq.at[0], sqx_in)
    along_x_all(0, qa_out.at[0], qax_in)
    along_z_all(1, qb_out.at[0], qbz_in)

    kv_part = jnp.concatenate([k_part, v_part], axis=1)
    for s in range(2):
        for j in range(4):
            kv_part_rows[pl.ds(4 * s + j, REQS, stride=8), :] = kv_part[
                s * REQS : s * REQS + REQS, j * HEAD : (j + 1) * HEAD
            ]
    for parity in range(2):
        kv_out[parity] = kv_part_rows[64 * parity : 64 * parity + 64, :].astype(BF16)

    @pl.loop(0, 3)
    def _(i):
        a = ring_peer(x, i, 4)
        send(12, kv_out.at[a % 2], kvx_in.at[i], (a * 8 + z, t))

    leaves(12, kvx_in)
    new_sq[1] = sum_of(11, new_sq.at[0], sqx_in)
    along_z_all(14, new_sq.at[1], sqz_in)
    qa_out[1] = sum_of(0, qa_out.at[0], qax_in).astype(BF16)
    along_z_all(13, qa_out.at[1], qaz_in)

    def transpose_keys(first):
        @pl.loop(first, first + 8)
        def _(r):
            kt[r] = kc[r].T

    loads[6].wait()
    transpose_keys(0)
    qb_out[1] = sum_of(1, qb_out.at[0], qbz_in).astype(BF16)
    along_x_all(15, qb_out.at[1], qbx_in)
    kv_sum[...] = sum_of(12, kv_out.at[x % 2], kvx_in)

    def kv_rows(place_z):
        local_request = lax.rem(place_z + 4 * (x // 2), 8)
        return kv_sum.at[pl.ds(pl.multiple_of(local_request * 8, 8), 8)]

    @pl.loop(0, 7)
    def _(i):
        b = ring_peer(z, i)
        send(16, kv_rows(b), kvz_in.at[i], (x * 8 + b, t))

    leaves(16, kvz_in)
    transpose_keys(8)
    squares = as_column(sum_of(14, new_sq.at[1], sqz_in))
    inv = lax.rsqrt(squares / WIDTH + EPS)
    inv_rows[...] = jnp.broadcast_to(inv, (ROWS, HEAD))
    part_b = sum_of(15, qb_out.at[1], qbx_in)
    part_a = sum_of(13, qa_out.at[1], qaz_in)
    totals = [part_a, part_b]
    for s in range(2):
        query = (totals[s] * inv[s * REQS : s * REQS + REQS]).astype(BF16).astype(F32)
        for j in range(4):
            start = (2 * j + s) * REQS
            qkv_all[start : start + REQS, :] = query[:, j * HEAD : (j + 1) * HEAD]

    loads[13].wait()
    loads[7].wait()
    lane = iota((8, 2 * POS), 1)
    own_head = (lane % 2) == (iota((8, 2 * POS), 0) // 4)
    position = c * POS + lane // 2

    lane = iota((8, HEAD), 1)
    for half in (NEAR[:8], NEAR[8:]):
        requests = [request_at(place(offset)) for offset in half]
        queries = [qkv_all[pl.ds(r, 8, stride=16), :].astype(BF16) for r in requests]
        scores = [jnp.dot(q, kt[r], preferred_element_type=F32) * SCALE for q, r in zip(queries, requests)]
        live = [own_head & (position < lengths[r]) for r in requests]
        peaks = [
            jnp.max(jnp.where(l, s, MASKED), axis=1, keepdims=True) for s, l in zip(scores, live)
        ]
        weights = [
            jnp.where(l, jnp.exp(s - m), 0.0) for s, l, m in zip(scores, live, peaks)
        ]
        sums = [jnp.sum(w, axis=1, keepdims=True) for w in weights]
        mixtures = [
            jnp.dot(w.astype(BF16), vc[r], preferred_element_type=F32)
            for w, r in zip(weights, requests)
        ]
        for r, m, total, mixture in zip(requests, peaks, sums, mixtures):
            first = m.astype(BF16).astype(F32)
            second = (m - first).astype(BF16).astype(F32)
            total_first = total.astype(BF16).astype(F32)
            stats = jnp.where(lane == 3, total_first, total - total_first)
            stats = jnp.where(lane == 2, m - first - second, stats)
            stats = jnp.where(lane == 1, second, stats)
            stats = jnp.where(lane == 0, first, stats)
            stats = jnp.where(lane > 4, 0.0, stats)
            mix_out[r] = jnp.concatenate([mixture, stats], axis=0).astype(BF16)
        for offset in far_first(half + [opposite(offset) for offset in half]):
            if offset != (0, 0):
                a, b = place(offset)
                send(2, mix_out.at[request_at((a, b))], mix_in.at[c], (a * 8 + b, t))

    leaves(2, mix_in.at[pl.ds(0, CTX - 1)])

    request = request_at((x, z))
    mix_in[c] = mix_out[request]
    query = qkv_all[pl.ds(request, 8, stride=16), :]
    first_head = iota((8, 1), 0) < 4
    second_step = (iota((8, 1), 0) % 2) == 1
    inv_step = [inv_rows[pl.ds(s * REQS + request, 1), :] for s in range(2)]
    new = sum_of(16, kv_rows(z), kvz_in) * jnp.where(first_head, inv_step[0], inv_step[1])
    new = new.astype(BF16).astype(F32)

    def new_rows(j, s):
        return jnp.where(first_head, new[4 * s + j : 4 * s + j + 1], new[4 * s + j + 1 : 4 * s + j + 2])

    own = [jnp.sum(query * new_rows(0, s), axis=1, keepdims=True) * SCALE for s in range(2)]
    own[1] = jnp.where(second_step, own[1], MASKED)
    new_values = [new_rows(2, s) for s in range(2)]
    wait(recv_sem.at[2], mix_in.at[pl.ds(0, CTX - 1)])
    mixed = mix_in[:, 0:8, :].astype(F32)
    stats = mix_in[:, 8:16, :].astype(F32)
    lane = iota((CTX, 8, HEAD), 2)
    peaks = jnp.sum(jnp.where(lane < 3, stats, 0.0), axis=2, keepdims=True)
    sums = jnp.sum(jnp.where(lane < 3, 0.0, stats), axis=2, keepdims=True)
    highest = jnp.maximum(jnp.max(peaks, axis=0), jnp.maximum(own[0], own[1]))
    rescale = jnp.exp(peaks - highest[None])
    denominator = jnp.sum(rescale * sums, axis=0)
    numerator = jnp.sum(rescale * mixed, axis=0)
    own_weight = [
        jnp.exp(own[0] - highest),
        jnp.where(second_step, jnp.exp(own[1] - highest), 0.0),
    ]
    for s in range(2):
        denominator = denominator + own_weight[s]
        numerator = numerator + own_weight[s] * new_values[s]
    mine = att_all.at[pl.ds(pl.multiple_of(request * 8, 8), 8)]
    mine[...] = (numerator / denominator).astype(BF16).astype(F32)
    for offset in far_first(NEAR):
        if offset != (0, 0):
            a, b = place(offset)
            send(3, mine, mine, (a * 8 + b, t))

    leaves(3, att_all.at[pl.ds(0, 8 * (REQS - 1))])
    loads[8].wait()
    wait(recv_sem.at[3], att_all.at[pl.ds(0, 8 * (REQS - 1))])

    att = jnp.concatenate(
        [
            jnp.concatenate(
                [
                    att_all[pl.ds(2 * j + s, REQS, stride=8), :]
                    for s in range(2)
                ],
                axis=0,
            )
            for j in range(4)
        ],
        axis=1,
    ).astype(BF16)
    pad = jnp.zeros((ROWS, 2 * HEAD - COLS), F32)

    def over_tensor(phase, value, slots):
        proj_out[phase - 4] = jnp.concatenate([value, pad], axis=1).astype(BF16)

        @pl.loop(0, TEN - 1)
        def _(i):
            send(phase, proj_out.at[phase - 4], slots.at[t], (c, ring_peer(t, i)))

        if phase == 5:
            while left:
                left.pop(0)()
        leaves(phase, slots.at[pl.ds(0, TEN - 1)])

        slots[t] = proj_out[phase - 4]
        wait(recv_sem.at[phase], slots.at[pl.ds(0, TEN - 1)])
        return jnp.sum(slots[...].astype(F32), axis=0)[:, 0:COLS]

    residual = rows + over_tensor(4, nt_dot(att, wo[...]), proj_in)

    square = jnp.sum(residual * residual, axis=1, keepdims=True)
    sq_out[0] = as_row(square)
    along_x_all(6, sq_out.at[0], sqfx_in)

    loads[12].wait()
    loads[14].wait()
    ffn_gated = (residual * gain2[...].astype(F32)[None, :]).astype(BF16)
    loads[9].wait()
    loads[10].wait()

    def partial(k, tiles):
        columns = pl.ds(pl.multiple_of(k * 256, 256), HEAD * tiles)
        gate = jnp.dot(ffn_gated, wg[:, columns], preferred_element_type=F32).astype(BF16)
        up = jnp.dot(ffn_gated, wu[:, columns], preferred_element_type=F32).astype(BF16)
        for a in range(2 * tiles):
            rows_of, columns_of = slice(a % 2 * 16, a % 2 * 16 + 16), slice(a // 2 * HEAD, a // 2 * HEAD + HEAD)
            gu_out[4 * k + a, 0:16, :] = gate[rows_of, columns_of]
            gu_out[4 * k + a, 16:32, :] = up[rows_of, columns_of]

    def along_x(n, k, i):
        a = ring_peer(x, i, 4)
        pltpu.make_async_remote_copy(
            src_ref=gu_out.at[4 * k + a],
            dst_ref=gx_in.at[n, i],
            send_sem=gx_send.at[n],
            recv_sem=gx_recv.at[n],
            device_id=(a * 8 + z, t),
            device_id_type=MESH,
        ).start()

    @pl.loop(0, 8)
    def _(n):
        k = ring_peer(z, n)
        partial(k, 2)
        for i in range(3):
            along_x(k, k, i)

        @pl.when(k < 2)
        def _():
            partial(8 + k, 2)
            for i in range(3):
                along_x(8 + k, 8 + k, i)

        @pl.when(k == 2)
        def _():
            partial(10, 1)
            for i in range(3):

                @pl.when(ring_peer(x, i, 4) < 2)
                def _():
                    along_x(10, 10, i)

    sq_out[1] = sum_of(6, sq_out.at[0], sqfx_in)
    along_z_all(10, sq_out.at[1], sqfz_in)

    def x_sum(k):
        wait(gx_recv.at[k], gx_in.at[k])
        total = gu_out[4 * k + x].astype(F32)
        for i in range(3):
            total = total + gx_in[k, i].astype(F32)
        return total.astype(BF16)

    def to_owner(k, slot, send_from, recv_at):
        pltpu.make_async_remote_copy(
            src_ref=gz_out.at[k],
            dst_ref=slot,
            send_sem=send_from,
            recv_sem=recv_at,
            device_id=(x * 8 + k % 8, t),
            device_id_type=MESH,
        ).start()

    @pl.loop(0, 7)
    def _(n):
        k = ring_peer(z, n)
        gz_out[k] = x_sum(k)
        to_owner(k, gz_in.at[n], send_sem.at[7], recv_sem.at[7])

        @pl.when((k < 2) | ((k == 2) & (x < 2)))
        def _():
            gz_out[8 + k] = x_sum(8 + k)
            to_owner(8 + k, gz_in2.at[n], gz_send.at[k], recv_sem.at[8])

    gz_in[7] = x_sum(z)
    leaves(7, gz_in.at[pl.ds(0, 7)])
    extra = (z < 2) | ((z == 2) & (x < 2))

    @pl.when(extra)
    def _():
        gz_in2[7] = x_sum(8 + z)

    def sent_extra():
        @pl.loop(0, 10)
        def _(k):
            wait(gx_send.at[k], gx_in.at[k])

        @pl.when(x < 2)
        def _():
            wait(gx_send.at[10], gx_in.at[10, pl.ds(0, 1)])

        @pl.when(x >= 2)
        def _():
            wait(gx_send.at[10], gx_in.at[10, pl.ds(0, 2)])

        for k in range(3):

            @pl.when(((x < 4) if k < 2 else (x < 2)) & (z != k))
            def _():
                wait(gz_send.at[k], gz_out.at[8 + k])

    left.append(sent_extra)

    squares = sum_of(10, sq_out.at[1], sqfz_in)
    step_rows = iota((REQS, HEAD), 1) == iota((REQS, HEAD), 0) + REQS * (x % 2)
    squares = jnp.sum(jnp.where(step_rows, squares, 0.0), axis=1, keepdims=True)
    ffn_inv = lax.rsqrt(squares / WIDTH + EPS)
    levels = jnp.zeros((REQS, 1), jnp.int32)
    for r in range(REQS):
        levels = jnp.where(iota((REQS, 1), 0) == r, granularity[r], levels)
    active = levels > t

    def hidden_of(slots):
        both = jnp.sum(slots[...].astype(F32), axis=0)
        gate = both[0:16] * ffn_inv
        up = both[16:32] * ffn_inv
        act = 0.5 * gate * (1.0 + jnp.tanh(GELU * (gate + 0.044715 * (gate * gate * gate))))
        return jnp.where(active, act * up, 0.0).astype(BF16)

    owner = 4 * z + x

    def units(first, count):
        return hid_all.at[pl.ds(pl.multiple_of(first * 16, 16), count * 16)]

    def share(first, count):
        block = units(first, count)

        @pl.loop(0, CTX - 1)
        def _(i):
            send(9, block, block, (peer_of(x, z, i), t))

    @pl.when(extra)
    def _():
        wait(recv_sem.at[8], gz_in2.at[pl.ds(0, 7)])
        units(2 * owner + 1, 1)[...] = hidden_of(gz_in2)

    wait(recv_sem.at[7], gz_in.at[pl.ds(0, 7)])
    hidden_main = hidden_of(gz_in)

    @pl.when(extra)
    def _():
        units(2 * owner, 1)[...] = hidden_main
        share(2 * owner, 2)

    @pl.when(jnp.logical_not(extra))
    def _():
        units(owner + EXTRA, 1)[...] = hidden_main
        share(owner + EXTRA, 1)

    def hidden_left():
        @pl.when(extra)
        def _():
            wait(send_sem.at[9], kc.at[0, pl.ds(0, 32 * (CTX - 1))])

        @pl.when(jnp.logical_not(extra))
        def _():
            wait(send_sem.at[9], hid_all.at[pl.ds(0, 16 * (CTX - 1))])

    left.append(hidden_left)
    loads[11].wait()

    @pl.when(extra)
    def _():
        wait(recv_sem.at[9], hid_all.at[pl.ds(0, 16 * (CTX + EXTRA - 2))])

    @pl.when(jnp.logical_not(extra))
    def _():
        wait(recv_sem.at[9], hid_all.at[pl.ds(0, 16 * (CTX + EXTRA - 1))])

    def unit_at(unit):
        own = unit % CTX
        place = 2 * own + unit // CTX if own < EXTRA else own + EXTRA
        return hid_all[place * 16 : place * 16 + 16, :]

    hidden = jnp.concatenate(
        [
            jnp.concatenate([unit_at(2 * i), unit_at(2 * i + 1)], axis=0)
            for i in range(TILES)
        ],
        axis=1,
    )
    output = residual + over_tensor(5, nt_dot(hidden, wd[...]), down_in)
    out_ref[...] = output.astype(BF16)

    for sent in left:
        sent()


def per_device(
    first_input,
    second_input,
    attn_gain,
    query_weight,
    key_weight,
    value_weight,
    out_weight,
    ffn_gain,
    gate_weight,
    up_weight,
    down_weight,
    key_cache,
    value_cache,
    lengths,
    granularity,
):
    hbm = pl.BlockSpec(memory_space=pltpu.HBM)
    vmem = pl.BlockSpec(memory_space=pltpu.VMEM)
    V = pltpu.VMEM
    (both,) = pl.pallas_call(
        kernel,
        out_shape=(
            pltpu.VMEM((ROWS, COLS), BF16),
        ),
        in_specs=[hbm] * 15,
        out_specs=(vmem,),
        scratch_shapes=[
            pltpu.SMEM((REQS,), jnp.int32),
            pltpu.SMEM((REQS,), jnp.int32),
            V((REQS, COLS), BF16),
            V((REQS, COLS), BF16),
            V((COLS,), BF16),
            V((COLS,), BF16),
            V((COLS, 512), BF16),
            V((COLS, 256), BF16),
            V((COLS, 256), BF16),
            V((COLS, 512), BF16),
            V((COLS, 2688), BF16),
            V((COLS, 2688), BF16),
            V((COLS, 2688), BF16),
            V((REQS, 2 * POS, HEAD), BF16),
            V((REQS, 2 * POS, HEAD), BF16),
            V((REQS, HEAD, 2 * POS), BF16),
            V((2, REQS, 512), BF16),
            V((2, REQS, 512), BF16),
            V((3, REQS, 512), BF16),
            V((7, REQS, 512), BF16),
            V((7, REQS, 512), BF16),
            V((3, REQS, 512), BF16),
            V((REQS * 8, HEAD), F32),
            V((2, 64, HEAD), BF16),
            V((3, 64, HEAD), BF16),
            V((64, HEAD), F32),
            V((7, 8, HEAD), F32),
            V((ROWS, HEAD), F32),
            V((2, 1, HEAD), F32),
            V((3, 1, HEAD), F32),
            V((7, 1, HEAD), F32),
            V((REQS * 8, HEAD), F32),
            V((REQS, 16, HEAD), BF16),
            V((CTX, 16, HEAD), BF16),
            V((REQS * 8, HEAD), F32),
            V((2, ROWS, 2 * HEAD), BF16),
            V((TEN, ROWS, 2 * HEAD), BF16),
            V((2, 1, HEAD), F32),
            V((3, 1, HEAD), F32),
            V((7, 1, HEAD), F32),
            V((2 * TILES, 32, HEAD), BF16),
            V((11, 3, 32, HEAD), BF16),
            V((11, 32, HEAD), BF16),
            V((8, 32, HEAD), BF16),
            V((8, 32, HEAD), BF16),
            V((TILES * ROWS, HEAD), BF16),
            V((TEN, ROWS, 2 * HEAD), BF16),
            pltpu.SemaphoreType.DMA((15,)),
            pltpu.SemaphoreType.DMA((17,)),
            pltpu.SemaphoreType.DMA((17,)),
            pltpu.SemaphoreType.DMA((11,)),
            pltpu.SemaphoreType.DMA((11,)),
            pltpu.SemaphoreType.DMA((3,)),
        ],
        compiler_params=pltpu.CompilerParams(
            collective_id=0, has_side_effects=True, vmem_limit_bytes=56 * 2**20
        ),
    )(
        lengths,
        granularity,
        first_input,
        second_input,
        attn_gain,
        ffn_gain,
        query_weight,
        key_weight,
        value_weight,
        out_weight.T,
        gate_weight,
        up_weight,
        down_weight.T,
        key_cache.reshape(REQS, 2 * POS, HEAD),
        value_cache.reshape(REQS, 2 * POS, HEAD),
    )
    return both[0:REQS], both[REQS:ROWS]


def solution(mesh):
    return jax.shard_map(
        per_device,
        mesh=mesh,
        in_specs=(
            P(None, "context"),
            P(None, "context"),
            P("context"),
            P("context", "tensor"),
            P("context", "tensor"),
            P("context", "tensor"),
            P("tensor", "context"),
            P("context"),
            P("context", "tensor"),
            P("context", "tensor"),
            P("tensor", "context"),
            P(None, "context", "tensor", None),
            P(None, "context", "tensor", None),
            P(),
            P(),
        ),
        out_specs=(P(None, "context"), P(None, "context")),
        check_vma=False,
    )
```
